32 devices in a mesh: groups: 2 (over x), row: 8 (over z, y), col: 2 (over core).
Axes of the slice: x: 2, y: 2, z: 4, core: 2. Of those that a mesh axis runs over, the one named last changes fastest.
Arguments:
- coefficients: bfloat16 [4096, 1000], P(('groups', 'row', 'col')), parts along dimension 0, may hold values from -0.375 to 0.375
- integrals: bfloat16 [4096, 8, 256], P(('groups', 'row', 'col')), parts along dimension 0, may hold values from -6 to 6
- send_blocks: int32 [32, 16, 2], P(('groups', 'row', 'col')), parts along dimension 0, may hold values from 0 to 15
- send_count: int32 [32, 16], P(('groups', 'row', 'col')), parts along dimension 0, may hold values from 1 to 2
Outputs:
- kband: float32 [4096, 640], P(('groups', 'row', 'col')), parts along dimension 0
The draws below stay inside these ranges and needn't reach their ends.
There are 2 independent parts, one for each index of `groups`. The reference program is written for one: setup_inputs(seed, part) draws one part's arguments, and reference() takes and returns one part's arrays. A program takes and returns all parts, laid end to end along the dimension named above; each array names one. Nothing has to cross between parts.
Inputs may be any that keep to these rules, and one draw needn't show every extreme that they name: `send_blocks`: block numbers within one owner's tile. Slot s carries data when s < send_count; some owner fills all 2 slots to some tile.
All inputs are finite; a program needn't handle non-finite values.
Results may differ from the reference program's by a relative error of at most 0.00098.
Values may be sent and summed in bfloat16 or wider, within the bound.
A program may use at most 64 MiB of HBM per device.

```python
import math
import jax
import jax.numpy as jnp
from jax import lax

OCC = 1000
TILE = 128
KB = 8
SLOT = 2
AUXB = 8
BAND = 2
OWNERS = 16
NBASIS = 2048
LOCAL_BLK = 16
COLS = 256
WIDE = 640


def place_ends(entries, rng, low, high):
    longest = entries.shape.index(max(entries.shape))
    spots = []
    for shift in (0, 1):
        where = [jax.random.randint(jax.random.fold_in(rng, axis), (), 0, length) for axis, length in enumerate(entries.shape)]
        where[longest] = (where[longest] + shift) % entries.shape[longest]
        spots.append(tuple(where))
    return entries.at[spots[0]].set(low).at[spots[1]].set(high)


def block_levels(rng, shape, split, least, largest):
    level, own = 1.0, jax.random.fold_in(rng, 6)
    for dim, blocks in split:
        draws = jnp.exp(jax.random.uniform(jax.random.fold_in(own, dim), (blocks,), jnp.float32, least / len(split), largest / len(split)))
        level = level * jnp.repeat(draws, shape[dim] // blocks).reshape([-1 if axis == dim else 1 for axis in range(len(shape))])
    return level


def gaussian(stream_key, dims, width, bound, split=(), kind=jnp.bfloat16):
    drawn = jax.random.normal(stream_key, dims, jnp.float32) * width
    if len(split) > 0:
        drawn = block_levels(stream_key, dims, split, -0.22, 0.18) * drawn
    return jnp.clip(drawn, min=-bound, max=bound).astype(kind)


def setup_inputs(seed: int = 0, part: int = 0) -> dict:
    key_of = jax.random.split(jax.random.key(seed), 5)
    part_keys = jax.random.split(jax.random.fold_in(key_of[4], part), 5)
    return {
        "coefficients": gaussian(part_keys[0], (NBASIS, OCC), COLS ** -0.5, 0.375, ((0, 16),)),
        "integrals": gaussian(part_keys[1], (NBASIS, AUXB, COLS), 1.0, 6.0, ((0, 16),)),
        "send_blocks": place_ends(jax.random.randint(part_keys[2], (OWNERS, OWNERS, SLOT), 0, LOCAL_BLK), jax.random.fold_in(part_keys[2], 1), 0, LOCAL_BLK - 1).astype(jnp.int32),
        "send_count": place_ends(jax.random.randint(part_keys[3], (OWNERS, OWNERS), 1, SLOT + 1), jax.random.fold_in(part_keys[3], 1), 1, SLOT).astype(jnp.int32),
    }


def pair_block(left_rows, right_rows, norm_scale):
    product = lax.dot_general(left_rows, right_rows, (((1,), (1,)), ((), ())), preferred_element_type=jnp.float32)
    return product * norm_scale

def reference(coefficients, integrals, send_blocks, send_count):
    owned = coefficients.reshape(OWNERS, LOCAL_BLK, KB, OCC)
    slot_ids = jnp.arange(SLOT, dtype=jnp.int32)

    def received_for(dest_index):
        chosen = jax.vmap(lambda blocks_of, chosen_ids: blocks_of[chosen_ids])(owned, send_blocks[:, dest_index, :])
        live_mask = slot_ids[None, :] < send_count[:, dest_index][:, None]
        chosen = jnp.where(live_mask[:, :, None, None], chosen, jnp.zeros((), chosen.dtype))
        return chosen.reshape(COLS, OCC)

    def half_for(dest_index):
        local_ints = lax.dynamic_slice_in_dim(integrals, (dest_index * TILE).astype(jnp.int32), TILE, 0)
        product = jnp.dot(local_ints.reshape(TILE * AUXB, COLS), received_for(dest_index), preferred_element_type=jnp.float32)
        return product.astype(jnp.bfloat16).reshape(TILE, AUXB * OCC)
    tile_ids = jnp.arange(OWNERS, dtype=jnp.int32)
    half_tiles = lax.map(half_for, tile_ids)
    norm_scale = 1.0 / math.sqrt(AUXB * OCC)
    border = jnp.zeros((BAND, TILE, AUXB * OCC), half_tiles.dtype)
    padded = jnp.concatenate([border, half_tiles, border], axis=0)

    def band_for(row_index):
        own_tile = lax.dynamic_index_in_dim(half_tiles, row_index, 0, keepdims=False)
        blocks_row = []
        for offset in range(-BAND, BAND + 1):
            other = lax.dynamic_index_in_dim(padded, row_index + BAND + offset, 0, keepdims=False)
            blocks_row.append(pair_block(own_tile, other, norm_scale))
        return jnp.concatenate(blocks_row, axis=1)
    banded = lax.map(band_for, tile_ids)
    return banded.reshape(NBASIS, WIDE)
```

```python
import functools
import math

import jax
import jax.numpy as jnp
from jax import lax
from jax.experimental import pallas as pl
from jax.experimental.pallas import tpu as pltpu
from jax.sharding import PartitionSpec as P

KB = 8
BAND = 2
LANES = 128
PARTS = 2
NEED = 3


def from_behind(array, axis, by):
    devices = lax.axis_size(axis)
    pairs = [(i, i + by) for i in range(devices) if 0 <= i + by < devices]
    return lax.ppermute(array, axis, pairs)


def pair_block(left_rows, right_rows, norm_scale):
    product = lax.dot_general(
        left_rows, right_rows, (((1,), (1,)), ((), ())), preferred_element_type=jnp.float32
    )
    return product * norm_scale


def general_body(coefficients, integrals, send_blocks, send_count):
    tile_rows = integrals.shape[0]
    aux_count = integrals.shape[1]
    column_total = integrals.shape[2]
    occ_count = coefficients.shape[1]
    slot_count = send_blocks.shape[2]
    owned_blocks = coefficients.reshape(tile_rows // KB, KB, occ_count)
    picked = jnp.take(owned_blocks, send_blocks[0], axis=0)
    live_mask = jnp.arange(slot_count, dtype=jnp.int32)[None, :] < send_count[0][:, None]
    outgoing = jnp.where(live_mask[:, :, None, None], picked, jnp.zeros((), picked.dtype))
    incoming = lax.all_to_all(outgoing, ("row", "col"), split_axis=0, concat_axis=0, tiled=True)
    received = incoming.reshape(column_total, occ_count)
    product = jnp.dot(
        integrals.reshape(tile_rows * aux_count, column_total),
        received,
        preferred_element_type=jnp.float32,
    )
    half_tiles = product.astype(jnp.bfloat16).reshape(tile_rows, aux_count * occ_count)
    norm_scale = 1.0 / math.sqrt(aux_count * occ_count)
    upper_blocks = []
    lower_blocks = []
    for offset in range(1, BAND + 1):
        above_tiles = from_behind(half_tiles, ("row", "col"), -offset)
        upper_blocks.append(pair_block(half_tiles, above_tiles, norm_scale))
        below_tiles = from_behind(half_tiles, ("row", "col"), offset)
        lower_blocks.append(pair_block(half_tiles, below_tiles, norm_scale))
    diagonal = pair_block(half_tiles, half_tiles, norm_scale)
    banded = jnp.concatenate(lower_blocks[::-1] + [diagonal] + upper_blocks, axis=1)
    return banded


def kernel(
    rows, occ, aux, scale,
    coef_ref, ints_ref, out_ref,
    coefs, held, stage, picked, sent, landed,
    own_sem, ring_send, ring_recv, pair_send, pair_recv, int_send, int_recv, res_send, res_recv,
):
    tiles = 2 * rows
    depth = rows // 2
    steps = rows - 1
    row, col = lax.axis_index("row"), lax.axis_index("col")
    me = 2 * row + col
    spot = jnp.where(row % 2 == 0, row // 2, rows - 1 - row // 2)
    padded = coef_ref.shape[0]
    part_rows = padded // PARTS
    tile = coef_ref.shape[1]
    own_rows = tile // KB

    def row_at(where):
        where = lax.rem(where + 2 * rows, rows)
        return jnp.where(where < depth, 2 * where, 2 * (rows - 1 - where) + 1)

    def device(which):
        return {"row": which // 2, "col": which % 2}

    partner = 2 * row + 1 - col
    right = 2 * row_at(spot + 1) + col
    left = 2 * row_at(spot - 1) + col
    skip = jnp.where(col == 0, 2, -2)
    others = (me, me + 1, me + skip)
    has_next = me + 1 < tiles
    has_prev = me >= 1
    has_skip = jnp.logical_and(me + skip >= 0, me + skip < tiles)
    has_back = jnp.logical_and(me - skip >= 0, me - skip < tiles)

    barrier = pltpu.get_barrier_semaphore()
    for step in range(1, tiles):
        pl.semaphore_signal(
            barrier, inc=1, device_id=device(lax.rem(me + step, tiles)),
            device_id_type=pl.DeviceIdType.MESH,
        )

    own = pltpu.make_async_copy(coef_ref, coefs.at[me], own_sem)
    own.start()
    own.wait()
    pl.semaphore_wait(barrier, tiles - 1)

    def remote(src, dst, send_sem, recv_sem, which):
        return pltpu.make_async_remote_copy(
            src_ref=src, dst_ref=dst, send_sem=send_sem, recv_sem=recv_sem,
            device_id=device(which), device_id_type=pl.DeviceIdType.MESH,
        )

    def piece(owner, part):
        return coefs.at[owner, pl.ds(part * part_rows, part_rows)]

    def ring(way, step):
        back = -(step // 2) if way == 0 else step // 2
        part = step % 2 if way == 0 else 1 - step % 2
        ref = piece(2 * row_at(spot + back) + col, part)
        return remote(ref, ref, ring_send.at[way, step], ring_recv.at[way, step], right if way == 0 else left)

    def arrival(way, step):
        back = -(step // 2) - 1 if way == 0 else step // 2 + 1
        part = step % 2 if way == 0 else 1 - step % 2
        ref = piece(2 * row_at(spot + back) + col, part)
        return remote(ref, ref, ring_send.at[way, step], ring_recv.at[way, step], right if way == 0 else left)

    def share(way, step, core):
        back = -(step // 2) - 1 if way == 0 else step // 2 + 1
        part = step % 2 if way == 0 else 1 - step % 2
        ref = piece(2 * row_at(spot + back) + core, part)
        return remote(ref, ref, pair_send.at[way, step], pair_recv.at[way, step], partner)

    def share_own(core):
        ref = coefs.at[2 * row + core]
        return remote(ref, ref, pair_send.at[0, steps], pair_recv.at[0, steps], partner)

    for step in range(2):
        for way in range(2):
            ring(way, step).start()
    share_own(col).start()

    for q in range(ints_ref.shape[1] // LANES):
        stage[q] = ints_ref[:, q * LANES:(q + 1) * LANES].astype(jnp.float32)
        for p in range(aux):
            lines = stage[q, pl.ds(p, tile, stride=aux), :]
            held[0, p, :, q * LANES:(q + 1) * LANES] = lines.astype(held.dtype)

    back_copy = remote(held.at[0], held.at[2], int_send.at[0], int_recv.at[1], me - skip)
    next_copy = remote(held.at[0], held.at[1], int_send.at[1], int_recv.at[0], partner)
    pass_copy = remote(held.at[2], held.at[1], int_send.at[1], int_recv.at[0], partner)

    @pl.when(has_back)
    def _():
        back_copy.start()

    @pl.when(col == 1)
    def _():
        next_copy.start()

    height = 2 * KB
    lane = lax.broadcasted_iota(jnp.int32, (height, LANES), 1)
    line = lax.broadcasted_iota(jnp.int32, (height, LANES), 0)
    number = lax.broadcasted_iota(jnp.int32, (NEED * height, LANES), 1).astype(jnp.float32)
    inner = (lax.broadcasted_iota(jnp.int32, (NEED * height, LANES), 0) % KB).astype(jnp.float32)
    occ_lane = lax.broadcasted_iota(jnp.int32, (NEED * height, LANES), 1)
    last = padded - LANES

    def pick(owner):
        meta = coefs[owner, pl.ds(padded - 16, 16), :].astype(jnp.float32)
        first = jnp.broadcast_to(meta[8:9], (height, LANES))
        second = jnp.broadcast_to(meta[9:10], (height, LANES))
        both = jnp.where(line < KB, first, second)
        chosen = jnp.concatenate(
            [
                jnp.sum(jnp.where(lane == other, both, 0.0), axis=1, keepdims=True)
                for other in others
            ],
            axis=0,
        )
        hot = (number == chosen * KB + inner).astype(jnp.float32).astype(coefs.dtype)
        got = lax.dot_general(
            hot, coefs[owner], (((1,), (1,)), ((), ())), preferred_element_type=jnp.float32
        )
        tail = jnp.where(occ_lane + last < occ, got[:, last:], 0.0)
        got = got.astype(picked.dtype)
        tail = tail.astype(picked.dtype)
        for k in range(NEED):
            rows_of = pl.ds(pl.multiple_of(owner * height, height), height)
            picked[k, rows_of, 0:last] = got[k * height:(k + 1) * height, 0:last]
            picked[k, rows_of, last:padded] = tail[k * height:(k + 1) * height]

    pick(me)
    for step in range(steps):
        for way in range(2):
            arrival(way, step).wait_recv()
            if step + 2 < steps:
                ring(way, step + 2).start()
            share(way, step, col).start()
        if step == 0:
            share_own(1 - col).wait_recv()
            pick(partner)
        if step % 2 == 1:
            for way in range(2):
                back = -(step // 2) - 1 if way == 0 else step // 2 + 1
                pick(2 * row_at(spot + back) + col)
            for way in range(2):
                for earlier in (step - 1, step):
                    share(way, earlier, 1 - col).wait_recv()
                back = -(step // 2) - 1 if way == 0 else step // 2 + 1
                pick(2 * row_at(spot + back) + 1 - col)
    opposite = row_at(spot + depth)
    pick(2 * opposite + col)

    @pl.when(has_skip)
    def _():
        remote(held.at[0], held.at[2], int_send.at[0], int_recv.at[1], me - skip).wait_recv()

    @pl.when(jnp.logical_and(col == 0, has_skip))
    def _():
        pass_copy.start()

    for way in range(2):
        share(way, steps - 1, 1 - col).wait_recv()
    pick(2 * opposite + 1 - col)

    @pl.when(has_next)
    def _():
        next_copy.wait_recv()

    def add_up(p, totals):
        halves = [
            jnp.dot(held[k, p], picked[k], preferred_element_type=jnp.float32).astype(jnp.bfloat16)
            for k in range(NEED)
        ]
        return tuple(
            total + lax.dot_general(
                halves[0], half, (((1,), (1,)), ((), ())), preferred_element_type=jnp.float32
            )
            for total, half in zip(totals, halves)
        )

    zero = jnp.zeros((tile, tile), jnp.float32)
    diag, above, far = lax.fori_loop(0, aux, add_up, (zero,) * NEED)
    above = above * scale
    far = far * scale
    out_ref[...] = jnp.zeros_like(out_ref)
    sent[0] = above.T
    sent[1] = far.T
    give_next = remote(sent.at[0], landed.at[0], res_send.at[0], res_recv.at[0], me + 1)
    give_skip = remote(sent.at[1], landed.at[1], res_send.at[1], res_recv.at[1], me + skip)

    @pl.when(has_next)
    def _():
        give_next.start()

    @pl.when(has_skip)
    def _():
        give_skip.start()

    out_ref[:, 2 * tile:3 * tile] = diag * scale

    @pl.when(has_next)
    def _():
        out_ref[:, 3 * tile:4 * tile] = above

    @pl.when(jnp.logical_and(has_skip, col == 0))
    def _():
        out_ref[:, 4 * tile:5 * tile] = far

    @pl.when(jnp.logical_and(has_skip, col == 1))
    def _():
        out_ref[:, 0:tile] = far

    for step in range(steps):
        for way in range(2):
            ring(way, step).wait_send()
            share(way, step, col).wait_send()
    share_own(col).wait_send()

    @pl.when(has_back)
    def _():
        back_copy.wait_send()

    @pl.when(col == 1)
    def _():
        next_copy.wait_send()

    @pl.when(jnp.logical_and(col == 0, has_skip))
    def _():
        pass_copy.wait_send()

    @pl.when(has_prev)
    def _():
        give_next.wait_recv()
        out_ref[:, tile:2 * tile] = landed[0]

    @pl.when(has_back)
    def _():
        give_skip.wait_recv()

    @pl.when(jnp.logical_and(has_back, col == 0))
    def _():
        out_ref[:, 0:tile] = landed[1]

    @pl.when(jnp.logical_and(has_back, col == 1))
    def _():
        out_ref[:, 4 * tile:5 * tile] = landed[1]

    @pl.when(has_next)
    def _():
        give_next.wait_send()

    @pl.when(has_skip)
    def _():
        give_skip.wait_send()


def ring_body(rows, coefficients, integrals, send_blocks, send_count):
    tile, aux, columns = integrals.shape
    occ = coefficients.shape[1]
    slots = send_blocks.shape[2]
    tiles = 2 * rows
    live = jnp.arange(slots, dtype=jnp.int32)[:, None] < send_count
    chosen = jnp.where(live, send_blocks[0].T, -1).astype(coefficients.dtype)
    padded = -(-(occ + slots) // LANES) * LANES
    meta_at = padded - 8
    flipped = jnp.pad(coefficients.T, ((0, padded - occ), (0, 0)))
    flipped = flipped + jnp.pad(chosen, ((meta_at, padded - meta_at - slots), (0, tile - tiles)))
    steps = rows - 1
    bf16, f32 = jnp.bfloat16, jnp.float32
    return pl.pallas_call(
        functools.partial(kernel, rows, occ, aux, 1.0 / math.sqrt(aux * occ)),
        out_shape=jax.ShapeDtypeStruct((tile, (2 * BAND + 1) * tile), f32),
        in_specs=[pl.BlockSpec(memory_space=pltpu.VMEM)] * 2,
        out_specs=pl.BlockSpec(memory_space=pltpu.VMEM),
        scratch_shapes=[
            pltpu.VMEM((tiles, padded, tile), bf16),
            pltpu.VMEM((NEED, aux, tile, columns), bf16),
            pltpu.VMEM((columns // LANES, tile * aux, LANES), f32),
            pltpu.VMEM((NEED, columns, padded), bf16),
            pltpu.VMEM((2, tile, tile), f32),
            pltpu.VMEM((2, tile, tile), f32),
            pltpu.SemaphoreType.DMA,
            pltpu.SemaphoreType.DMA((2, steps)),
            pltpu.SemaphoreType.DMA((2, steps)),
            pltpu.SemaphoreType.DMA((2, steps + 1)),
            pltpu.SemaphoreType.DMA((2, steps + 1)),
            pltpu.SemaphoreType.DMA((2,)),
            pltpu.SemaphoreType.DMA((2,)),
            pltpu.SemaphoreType.DMA((2,)),
            pltpu.SemaphoreType.DMA((2,)),
        ],
        compiler_params=pltpu.CompilerParams(
            collective_id=0, has_side_effects=True, vmem_limit_bytes=40 * 1024 * 1024
        ),
    )(flipped, integrals.reshape(tile * aux, columns))


def solution(mesh):
    rows, cols = mesh.shape["row"], mesh.shape["col"]
    if cols == 2 and rows % 2 == 0 and 4 <= rows <= 8:
        body = functools.partial(ring_body, rows)
    else:
        body = general_body
    return jax.shard_map(
        body,
        mesh=mesh,
        in_specs=(
            P(("groups", "row", "col"), None),
            P(("groups", "row", "col"), None, None),
            P(("groups", "row", "col"), None, None),
            P(("groups", "row", "col"), None),
        ),
        out_specs=P(("groups", "row", "col"), None),
        check_vma=False,
    )
```

```python
import functools
import math

import jax
import jax.numpy as jnp
from jax import lax
from jax.experimental import pallas as pl
from jax.experimental.pallas import tpu as pltpu
from jax.sharding import PartitionSpec as P

KB = 8
BAND = 2
LANES = 128
PARTS = 2
NEED = 3


def from_behind(array, axis, by):
    devices = lax.axis_size(axis)
    pairs = [(i, i + by) for i in range(devices) if 0 <= i + by < devices]
    return lax.ppermute(array, axis, pairs)


def pair_block(left_rows, right_rows, norm_scale):
    product = lax.dot_general(
        left_rows, right_rows, (((1,), (1,)), ((), ())), preferred_element_type=jnp.float32
    )
    return product * norm_scale


def general_body(coefficients, integrals, send_blocks, send_count):
    tile_rows = integrals.shape[0]
    aux_count = integrals.shape[1]
    column_total = integrals.shape[2]
    occ_count = coefficients.shape[1]
    slot_count = send_blocks.shape[2]
    owned_blocks = coefficients.reshape(tile_rows // KB, KB, occ_count)
    picked = jnp.take(owned_blocks, send_blocks[0], axis=0)
    live_mask = jnp.arange(slot_count, dtype=jnp.int32)[None, :] < send_count[0][:, None]
    outgoing = jnp.where(live_mask[:, :, None, None], picked, jnp.zeros((), picked.dtype))
    incoming = lax.all_to_all(outgoing, ("row", "col"), split_axis=0, concat_axis=0, tiled=True)
    received = incoming.reshape(column_total, occ_count)
    product = jnp.dot(
        integrals.reshape(tile_rows * aux_count, column_total),
        received,
        preferred_element_type=jnp.float32,
    )
    half_tiles = product.astype(jnp.bfloat16).reshape(tile_rows, aux_count * occ_count)
    norm_scale = 1.0 / math.sqrt(aux_count * occ_count)
    upper_blocks = []
    lower_blocks = []
    for offset in range(1, BAND + 1):
        above_tiles = from_behind(half_tiles, ("row", "col"), -offset)
        upper_blocks.append(pair_block(half_tiles, above_tiles, norm_scale))
        below_tiles = from_behind(half_tiles, ("row", "col"), offset)
        lower_blocks.append(pair_block(half_tiles, below_tiles, norm_scale))
    diagonal = pair_block(half_tiles, half_tiles, norm_scale)
    banded = jnp.concatenate(lower_blocks[::-1] + [diagonal] + upper_blocks, axis=1)
    return banded


def kernel(
    rows, occ, aux, scale,
    coef_ref, ints_ref, blocks_ref, count_ref, out_ref,
    coefs, notes, held, stage, picked, sent, landed,
    ring_send, ring_recv, pair_send, pair_recv, int_send, int_recv, res_send, res_recv,
):
    tiles = 2 * rows
    depth = rows // 2
    steps = rows - 1
    row, col = lax.axis_index("row"), lax.axis_index("col")
    me = 2 * row + col
    spot = jnp.where(row % 2 == 0, row // 2, rows - 1 - row // 2)
    padded = coefs.shape[1]
    part_rows = padded // PARTS
    tile = coef_ref.shape[1]
    own_rows = tile // KB

    def row_at(where):
        where = lax.rem(where + 2 * rows, rows)
        return jnp.where(where < depth, 2 * where, 2 * (rows - 1 - where) + 1)

    def device(which):
        return {"row": which // 2, "col": which % 2}

    partner = 2 * row + 1 - col
    right = 2 * row_at(spot + 1) + col
    left = 2 * row_at(spot - 1) + col
    skip = jnp.where(col == 0, 2, -2)
    others = (me, me + 1, me + skip)
    has_next = me + 1 < tiles
    has_prev = me >= 1
    has_skip = jnp.logical_and(me + skip >= 0, me + skip < tiles)
    has_back = jnp.logical_and(me - skip >= 0, me - skip < tiles)

    barrier = pltpu.get_barrier_semaphore()

    def greet(which):
        pl.semaphore_signal(
            barrier, inc=1, device_id=device(which), device_id_type=pl.DeviceIdType.MESH
        )

    cross = me - 1 + 2 * col
    has_cross = jnp.logical_and(cross >= 0, cross < tiles)
    for which in (left, right, partner):
        greet(which)
    for there, which in ((has_skip, me + skip), (has_back, me - skip), (has_cross, cross)):
        pl.when(there)(functools.partial(greet, which))

    slots, dests = blocks_ref.shape
    whole = occ // 16 * 16
    live = lax.broadcasted_iota(jnp.int32, (slots, dests), 0) < count_ref[...]
    notes[...] = jnp.zeros_like(notes)
    notes[0:slots, 0:dests] = jnp.where(live, blocks_ref[...], -1).astype(jnp.float32)
    coefs[me, 0:whole] = coef_ref[0:whole]
    rest = jnp.concatenate(
        [
            coef_ref[whole:occ].astype(jnp.float32),
            jnp.zeros((padded - 8 - occ, tile), jnp.float32),
            notes[...],
        ],
        axis=0,
    )
    coefs[me, whole:padded] = rest.astype(coefs.dtype)
    greeted = 3 + has_skip.astype(jnp.int32) + has_back.astype(jnp.int32) + has_cross.astype(jnp.int32)
    pl.semaphore_wait(barrier, greeted)

    def remote(src, dst, send_sem, recv_sem, which):
        return pltpu.make_async_remote_copy(
            src_ref=src, dst_ref=dst, send_sem=send_sem, recv_sem=recv_sem,
            device_id=device(which), device_id_type=pl.DeviceIdType.MESH,
        )

    def piece(owner, part):
        return coefs.at[owner, pl.ds(part * part_rows, part_rows)]

    def ring(way, step):
        back = -(step // 2) if way == 0 else step // 2
        part = step % 2 if way == 0 else 1 - step % 2
        ref = piece(2 * row_at(spot + back) + col, part)
        return remote(ref, ref, ring_send.at[way, step], ring_recv.at[way, step], right if way == 0 else left)

    def arrival(way, step):
        back = -(step // 2) - 1 if way == 0 else step // 2 + 1
        part = step % 2 if way == 0 else 1 - step % 2
        ref = piece(2 * row_at(spot + back) + col, part)
        return remote(ref, ref, ring_send.at[way, step], ring_recv.at[way, step], right if way == 0 else left)

    def share(way, step, core):
        back = -(step // 2) - 1 if way == 0 else step // 2 + 1
        part = step % 2 if way == 0 else 1 - step % 2
        ref = piece(2 * row_at(spot + back) + core, part)
        return remote(ref, ref, pair_send.at[way, step], pair_recv.at[way, step], partner)

    def share_own(core):
        ref = coefs.at[2 * row + core]
        return remote(ref, ref, pair_send.at[0, steps], pair_recv.at[0, steps], partner)

    for step in range(2):
        for way in range(2):
            ring(way, step).start()
    share_own(col).start()

    for q in range(ints_ref.shape[1] // LANES):
        stage[q] = ints_ref[:, q * LANES:(q + 1) * LANES].astype(jnp.float32)
        for p in range(aux):
            lines = stage[q, pl.ds(p, tile, stride=aux), :]
            held[0, p * tile:(p + 1) * tile, q * LANES:(q + 1) * LANES] = lines.astype(held.dtype)

    back_copy = remote(held.at[0], held.at[2], int_send.at[0], int_recv.at[1], me - skip)
    next_copy = remote(held.at[0], held.at[1], int_send.at[1], int_recv.at[0], partner)
    pass_copy = remote(held.at[2], held.at[1], int_send.at[1], int_recv.at[0], partner)

    @pl.when(has_back)
    def _():
        back_copy.start()

    @pl.when(col == 1)
    def _():
        next_copy.start()

    height = 2 * KB
    lane = lax.broadcasted_iota(jnp.int32, (height, LANES), 1)
    line = lax.broadcasted_iota(jnp.int32, (height, LANES), 0)
    number = lax.broadcasted_iota(jnp.int32, (NEED * height, LANES), 1).astype(jnp.float32)
    inner = (lax.broadcasted_iota(jnp.int32, (NEED * height, LANES), 0) % KB).astype(jnp.float32)
    occ_lane = lax.broadcasted_iota(jnp.int32, (NEED * height, LANES), 1)
    last = padded - LANES

    def pick(owner):
        meta = coefs[owner, pl.ds(padded - 16, 16), :].astype(jnp.float32)
        first = jnp.broadcast_to(meta[8:9], (height, LANES))
        second = jnp.broadcast_to(meta[9:10], (height, LANES))
        both = jnp.where(line < KB, first, second)
        chosen = jnp.concatenate(
            [
                jnp.sum(jnp.where(lane == other, both, 0.0), axis=1, keepdims=True)
                for other in others
            ],
            axis=0,
        )
        hot = (number == chosen * KB + inner).astype(jnp.float32).astype(coefs.dtype)
        got = lax.dot_general(
            hot, coefs[owner], (((1,), (1,)), ((), ())), preferred_element_type=jnp.float32
        )
        tail = jnp.where(occ_lane + last < occ, got[:, last:], 0.0)
        got = got.astype(picked.dtype)
        tail = tail.astype(picked.dtype)
        for k in range(NEED):
            rows_of = pl.ds(pl.multiple_of(owner * height, height), height)
            picked[k, rows_of, 0:last] = got[k * height:(k + 1) * height, 0:last]
            picked[k, rows_of, last:padded] = tail[k * height:(k + 1) * height]

    pick(me)
    for step in range(steps):
        for way in range(2):
            arrival(way, step).wait_recv()
            if step + 2 < steps:
                ring(way, step + 2).start()
            share(way, step, col).start()
        if step == 0:
            share_own(1 - col).wait_recv()
            pick(partner)
        if step % 2 == 1:
            for way in range(2):
                back = -(step // 2) - 1 if way == 0 else step // 2 + 1
                pick(2 * row_at(spot + back) + col)
            for way in range(2):
                for earlier in (step - 1, step):
                    share(way, earlier, 1 - col).wait_recv()
                back = -(step // 2) - 1 if way == 0 else step // 2 + 1
                pick(2 * row_at(spot + back) + 1 - col)
    opposite = row_at(spot + depth)
    pick(2 * opposite + col)

    @pl.when(has_skip)
    def _():
        remote(held.at[0], held.at[2], int_send.at[0], int_recv.at[1], me - skip).wait_recv()

    @pl.when(jnp.logical_and(col == 0, has_skip))
    def _():
        pass_copy.start()

    for way in range(2):
        share(way, steps - 1, 1 - col).wait_recv()
    pick(2 * opposite + 1 - col)

    @pl.when(has_next)
    def _():
        next_copy.wait_recv()

    group = 2

    def add_up(step, total):
        rows_of = pl.ds(pl.multiple_of(step * group * tile, group * tile), group * tile)
        halves = [
            jnp.dot(
                held[k, rows_of], picked[k], preferred_element_type=jnp.float32
            ).astype(jnp.bfloat16)
            for k in range(NEED)
        ]
        for p in range(group):
            slices = [half[p * tile:(p + 1) * tile] for half in halves]
            total = total + lax.dot_general(
                slices[0], jnp.concatenate(slices, axis=0),
                (((1,), (1,)), ((), ())), preferred_element_type=jnp.float32,
            )
        return total

    zero = jnp.zeros((tile, NEED * tile), jnp.float32)
    total = lax.fori_loop(0, aux // group, add_up, zero) * scale
    diag, above, far = (total[:, k * tile:(k + 1) * tile] for k in range(NEED))
    out_ref[...] = jnp.zeros_like(out_ref)
    sent[0] = above.T
    sent[1] = far.T
    give_next = remote(sent.at[0], landed.at[0], res_send.at[0], res_recv.at[0], me + 1)
    give_skip = remote(sent.at[1], landed.at[1], res_send.at[1], res_recv.at[1], me + skip)

    @pl.when(has_next)
    def _():
        give_next.start()

    @pl.when(has_skip)
    def _():
        give_skip.start()

    out_ref[:, 2 * tile:3 * tile] = diag

    @pl.when(has_next)
    def _():
        out_ref[:, 3 * tile:4 * tile] = above

    @pl.when(jnp.logical_and(has_skip, col == 0))
    def _():
        out_ref[:, 4 * tile:5 * tile] = far

    @pl.when(jnp.logical_and(has_skip, col == 1))
    def _():
        out_ref[:, 0:tile] = far

    for step in range(steps):
        for way in range(2):
            ring(way, step).wait_send()
            share(way, step, col).wait_send()
    share_own(col).wait_send()

    @pl.when(has_back)
    def _():
        back_copy.wait_send()

    @pl.when(col == 1)
    def _():
        next_copy.wait_send()

    @pl.when(jnp.logical_and(col == 0, has_skip))
    def _():
        pass_copy.wait_send()

    @pl.when(has_prev)
    def _():
        give_next.wait_recv()
        out_ref[:, tile:2 * tile] = landed[0]

    @pl.when(has_back)
    def _():
        give_skip.wait_recv()

    @pl.when(jnp.logical_and(has_back, col == 0))
    def _():
        out_ref[:, 0:tile] = landed[1]

    @pl.when(jnp.logical_and(has_back, col == 1))
    def _():
        out_ref[:, 4 * tile:5 * tile] = landed[1]

    @pl.when(has_next)
    def _():
        give_next.wait_send()

    @pl.when(has_skip)
    def _():
        give_skip.wait_send()


def ring_body(rows, coefficients, integrals, send_blocks, send_count):
    tile, aux, columns = integrals.shape
    occ = coefficients.shape[1]
    tiles = 2 * rows
    padded = -(-(occ + 8) // LANES) * LANES
    steps = rows - 1
    bf16, f32 = jnp.bfloat16, jnp.float32
    return pl.pallas_call(
        functools.partial(kernel, rows, occ, aux, 1.0 / math.sqrt(aux * occ)),
        out_shape=jax.ShapeDtypeStruct((tile, (2 * BAND + 1) * tile), f32),
        in_specs=[pl.BlockSpec(memory_space=pltpu.VMEM)] * 4,
        out_specs=pl.BlockSpec(memory_space=pltpu.VMEM),
        scratch_shapes=[
            pltpu.VMEM((tiles, padded, tile), bf16),
            pltpu.VMEM((8, tile), f32),
            pltpu.VMEM((NEED, aux * tile, columns), bf16),
            pltpu.VMEM((columns // LANES, tile * aux, LANES), f32),
            pltpu.VMEM((NEED, columns, padded), bf16),
            pltpu.VMEM((2, tile, tile), f32),
            pltpu.VMEM((2, tile, tile), f32),
            pltpu.SemaphoreType.DMA((2, steps)),
            pltpu.SemaphoreType.DMA((2, steps)),
            pltpu.SemaphoreType.DMA((2, steps + 1)),
            pltpu.SemaphoreType.DMA((2, steps + 1)),
            pltpu.SemaphoreType.DMA((2,)),
            pltpu.SemaphoreType.DMA((2,)),
            pltpu.SemaphoreType.DMA((2,)),
            pltpu.SemaphoreType.DMA((2,)),
        ],
        compiler_params=pltpu.CompilerParams(
            collective_id=0, has_side_effects=True, vmem_limit_bytes=40 * 1024 * 1024
        ),
    )(coefficients.T, integrals.reshape(tile * aux, columns), send_blocks[0].T, send_count)


def solution(mesh):
    rows, cols = mesh.shape["row"], mesh.shape["col"]
    if cols == 2 and rows % 2 == 0 and 4 <= rows <= 8:
        body = functools.partial(ring_body, rows)
    else:
        body = general_body
    return jax.shard_map(
        body,
        mesh=mesh,
        in_specs=(
            P(("groups", "row", "col"), None),
            P(("groups", "row", "col"), None, None),
            P(("groups", "row", "col"), None, None),
            P(("groups", "row", "col"), None),
        ),
        out_specs=P(("groups", "row", "col"), None),
        check_vma=False,
    )
```

```python
import functools
import math

import jax
import jax.numpy as jnp
from jax import lax
from jax.experimental import pallas as pl
from jax.experimental.pallas import tpu as pltpu
from jax.sharding import PartitionSpec as P

KB = 8
BAND = 2
LANES = 128
PARTS = 2
NEED = 3


def from_behind(array, axis, by):
    devices = lax.axis_size(axis)
    pairs = [(i, i + by) for i in range(devices) if 0 <= i + by < devices]
    return lax.ppermute(array, axis, pairs)


def pair_block(left_rows, right_rows, norm_scale):
    product = lax.dot_general(
        left_rows, right_rows, (((1,), (1,)), ((), ())), preferred_element_type=jnp.float32
    )
    return product * norm_scale


def general_body(coefficients, integrals, send_blocks, send_count):
    tile_rows = integrals.shape[0]
    aux_count = integrals.shape[1]
    column_total = integrals.shape[2]
    occ_count = coefficients.shape[1]
    slot_count = send_blocks.shape[2]
    owned_blocks = coefficients.reshape(tile_rows // KB, KB, occ_count)
    picked = jnp.take(owned_blocks, send_blocks[0], axis=0)
    live_mask = jnp.arange(slot_count, dtype=jnp.int32)[None, :] < send_count[0][:, None]
    outgoing = jnp.where(live_mask[:, :, None, None], picked, jnp.zeros((), picked.dtype))
    incoming = lax.all_to_all(outgoing, ("row", "col"), split_axis=0, concat_axis=0, tiled=True)
    received = incoming.reshape(column_total, occ_count)
    product = jnp.dot(
        integrals.reshape(tile_rows * aux_count, column_total),
        received,
        preferred_element_type=jnp.float32,
    )
    half_tiles = product.astype(jnp.bfloat16).reshape(tile_rows, aux_count * occ_count)
    norm_scale = 1.0 / math.sqrt(aux_count * occ_count)
    upper_blocks = []
    lower_blocks = []
    for offset in range(1, BAND + 1):
        above_tiles = from_behind(half_tiles, ("row", "col"), -offset)
        upper_blocks.append(pair_block(half_tiles, above_tiles, norm_scale))
        below_tiles = from_behind(half_tiles, ("row", "col"), offset)
        lower_blocks.append(pair_block(half_tiles, below_tiles, norm_scale))
    diagonal = pair_block(half_tiles, half_tiles, norm_scale)
    banded = jnp.concatenate(lower_blocks[::-1] + [diagonal] + upper_blocks, axis=1)
    return banded


def kernel(
    rows, aux, scale,
    coef_hbm, ints_hbm, blocks_hbm, count_hbm, out_ref,
    coef_ref, ints_ref, blocks_ref, count_ref, coefs, notes, held, relay, stage, picked, sent, landed,
    in_sem, ring_send, ring_recv, pair_send, pair_recv, int_send, int_recv, res_send, res_recv,
):
    fetches = [
        pltpu.make_async_copy(src, dst, in_sem.at[k])
        for k, (src, dst) in enumerate((
            (coef_hbm, coef_ref), (blocks_hbm, blocks_ref), (count_hbm, count_ref), (ints_hbm, ints_ref)
        ))
    ]
    for fetch in fetches:
        fetch.start()
    occ = coef_hbm.shape[0]
    tiles = 2 * rows
    depth = rows // 2
    steps = rows - 1
    row, col = lax.axis_index("row"), lax.axis_index("col")
    me = 2 * row + col
    spot = jnp.where(row % 2 == 0, row // 2, rows - 1 - row // 2)
    padded = coefs.shape[1]
    part_rows = padded // PARTS
    tile = coef_ref.shape[1]
    own_rows = tile // KB

    def row_at(where):
        where = lax.rem(where + 2 * rows, rows)
        return jnp.where(where < depth, 2 * where, 2 * (rows - 1 - where) + 1)

    def device(which):
        return {"row": which // 2, "col": which % 2}

    partner = 2 * row + 1 - col
    right = 2 * row_at(spot + 1) + col
    left = 2 * row_at(spot - 1) + col
    skip = jnp.where(col == 0, 2, -2)
    others = (me, me + 1, me + skip)
    has_next = me + 1 < tiles
    has_prev = me >= 1
    has_skip = jnp.logical_and(me + skip >= 0, me + skip < tiles)
    has_back = jnp.logical_and(me - skip >= 0, me - skip < tiles)

    barrier = pltpu.get_barrier_semaphore()

    def greet(which):
        pl.semaphore_signal(
            barrier, inc=1, device_id=device(which), device_id_type=pl.DeviceIdType.MESH
        )

    cross = me - 1 + 2 * col
    has_cross = jnp.logical_and(cross >= 0, cross < tiles)
    for which in (left, right, partner):
        greet(which)
    for there, which in ((has_skip, me + skip), (has_back, me - skip), (has_cross, cross)):
        pl.when(there)(functools.partial(greet, which))

    for fetch in fetches[:3]:
        fetch.wait()
    slots, dests = blocks_ref.shape
    whole = occ // 16 * 16
    live = lax.broadcasted_iota(jnp.int32, (slots, dests), 0) < count_ref[...]
    notes[...] = jnp.zeros_like(notes)
    notes[0:slots, 0:dests] = jnp.where(live, blocks_ref[...], -1).astype(jnp.float32)
    coefs[me, 0:whole] = coef_ref[0:whole]
    rest = jnp.concatenate(
        [
            coef_ref[whole:occ].astype(jnp.float32),
            jnp.zeros((padded - 8 - occ, tile), jnp.float32),
            notes[...],
        ],
        axis=0,
    )
    coefs[me, whole:padded] = rest.astype(coefs.dtype)
    greeted = 3 + has_skip.astype(jnp.int32) + has_back.astype(jnp.int32) + has_cross.astype(jnp.int32)
    pl.semaphore_wait(barrier, greeted)

    def remote(src, dst, send_sem, recv_sem, which):
        return pltpu.make_async_remote_copy(
            src_ref=src, dst_ref=dst, send_sem=send_sem, recv_sem=recv_sem,
            device_id=device(which), device_id_type=pl.DeviceIdType.MESH,
        )

    def piece(owner, part):
        return coefs.at[owner, pl.ds(part * part_rows, part_rows)]

    def ring(way, step):
        back = -(step // 2) if way == 0 else step // 2
        part = step % 2 if way == 0 else 1 - step % 2
        ref = piece(2 * row_at(spot + back) + col, part)
        return remote(ref, ref, ring_send.at[way, step], ring_recv.at[way, step], right if way == 0 else left)

    def arrival(way, step):
        back = -(step // 2) - 1 if way == 0 else step // 2 + 1
        part = step % 2 if way == 0 else 1 - step % 2
        ref = piece(2 * row_at(spot + back) + col, part)
        return remote(ref, ref, ring_send.at[way, step], ring_recv.at[way, step], right if way == 0 else left)

    def share(way, step, core):
        back = -(step // 2) - 1 if way == 0 else step // 2 + 1
        part = step % 2 if way == 0 else 1 - step % 2
        ref = piece(2 * row_at(spot + back) + core, part)
        return remote(ref, ref, pair_send.at[way, step], pair_recv.at[way, step], partner)

    def share_own(core):
        ref = coefs.at[2 * row + core]
        return remote(ref, ref, pair_send.at[0, steps], pair_recv.at[0, steps], partner)

    for step in range(2):
        for way in range(2):
            ring(way, step).start()
    share_own(col).start()

    fetches[3].wait()
    for q in range(ints_ref.shape[1] // LANES):
        stage[q] = ints_ref[:, q * LANES:(q + 1) * LANES].astype(jnp.float32)
        for p in range(aux):
            lines = stage[q, pl.ds(p, tile, stride=aux), :]
            held[0, p * tile:(p + 1) * tile, q * LANES:(q + 1) * LANES] = lines.astype(held.dtype)

    back_copy = remote(held.at[0], held.at[2], int_send.at[0], int_recv.at[1], me - skip)
    next_copy = remote(held.at[0], held.at[1], int_send.at[1], int_recv.at[0], partner)
    pass_copy = remote(held.at[2], held.at[1], int_send.at[1], int_recv.at[0], partner)

    detours = ((4, 6, 2), (tiles - 5, tiles - 7, tiles - 3))
    is_from = functools.reduce(jnp.logical_or, [me == way[0] for way in detours])
    is_via = functools.reduce(jnp.logical_or, [me == way[1] for way in detours])
    via = jnp.where(col == 0, detours[0][1], detours[1][1])
    end = jnp.where(col == 0, detours[0][2], detours[1][2])
    leave_copy = remote(held.at[0], relay, int_send.at[0], int_recv.at[2], via)
    relay_copy = remote(relay, held.at[2], int_send.at[2], int_recv.at[1], end)

    @pl.when(jnp.logical_and(has_back, jnp.logical_not(is_from)))
    def _():
        back_copy.start()

    @pl.when(is_from)
    def _():
        leave_copy.start()

    @pl.when(col == 1)
    def _():
        next_copy.start()

    height = 2 * KB
    lane = lax.broadcasted_iota(jnp.int32, (height, LANES), 1)
    line = lax.broadcasted_iota(jnp.int32, (height, LANES), 0)
    number = lax.broadcasted_iota(jnp.int32, (NEED * height, LANES), 1).astype(jnp.float32)
    inner = (lax.broadcasted_iota(jnp.int32, (NEED * height, LANES), 0) % KB).astype(jnp.float32)
    occ_lane = lax.broadcasted_iota(jnp.int32, (NEED * height, LANES), 1)
    last = padded - LANES

    def pick(owner):
        meta = coefs[owner, pl.ds(padded - 16, 16), :].astype(jnp.float32)
        first = jnp.broadcast_to(meta[8:9], (height, LANES))
        second = jnp.broadcast_to(meta[9:10], (height, LANES))
        both = jnp.where(line < KB, first, second)
        chosen = jnp.concatenate(
            [
                jnp.sum(jnp.where(lane == other, both, 0.0), axis=1, keepdims=True)
                for other in others
            ],
            axis=0,
        )
        hot = (number == chosen * KB + inner).astype(jnp.float32).astype(coefs.dtype)
        got = lax.dot_general(
            hot, coefs[owner], (((1,), (1,)), ((), ())), preferred_element_type=jnp.float32
        )
        tail = jnp.where(occ_lane + last < occ, got[:, last:], 0.0)
        got = got.astype(picked.dtype)
        tail = tail.astype(picked.dtype)
        for k in range(NEED):
            rows_of = pl.ds(pl.multiple_of(owner * height, height), height)
            picked[k, rows_of, 0:last] = got[k * height:(k + 1) * height, 0:last]
            picked[k, rows_of, last:padded] = tail[k * height:(k + 1) * height]

    pick(me)
    for step in range(steps):
        for way in range(2):
            arrival(way, step).wait_recv()
            if step + 2 < steps:
                ring(way, step + 2).start()
            share(way, step, col).start()
        if step == 2:
            @pl.when(is_via)
            def _():
                leave_copy.wait_recv()
                relay_copy.start()
        if step == 0:
            share_own(1 - col).wait_recv()
            pick(partner)
        if step % 2 == 1:
            for way in range(2):
                back = -(step // 2) - 1 if way == 0 else step // 2 + 1
                pick(2 * row_at(spot + back) + col)
            for way in range(2):
                for earlier in (step - 1, step):
                    share(way, earlier, 1 - col).wait_recv()
                back = -(step // 2) - 1 if way == 0 else step // 2 + 1
                pick(2 * row_at(spot + back) + 1 - col)
    opposite = row_at(spot + depth)
    pick(2 * opposite + col)

    @pl.when(has_skip)
    def _():
        remote(held.at[0], held.at[2], int_send.at[0], int_recv.at[1], me - skip).wait_recv()

    @pl.when(jnp.logical_and(col == 0, has_skip))
    def _():
        pass_copy.start()

    for way in range(2):
        share(way, steps - 1, 1 - col).wait_recv()
    pick(2 * opposite + 1 - col)

    @pl.when(has_next)
    def _():
        next_copy.wait_recv()

    group = 2

    def add_up(step, total):
        rows_of = pl.ds(pl.multiple_of(step * group * tile, group * tile), group * tile)
        halves = [
            jnp.dot(
                held[k, rows_of], picked[k], preferred_element_type=jnp.float32
            ).astype(jnp.bfloat16)
            for k in range(NEED)
        ]
        for p in range(group):
            slices = [half[p * tile:(p + 1) * tile] for half in halves]
            total = total + lax.dot_general(
                slices[0], jnp.concatenate(slices, axis=0),
                (((1,), (1,)), ((), ())), preferred_element_type=jnp.float32,
            )
        return total

    zero = jnp.zeros((tile, NEED * tile), jnp.float32)
    total = lax.fori_loop(0, aux // group, add_up, zero) * scale
    diag, above, far = (total[:, k * tile:(k + 1) * tile] for k in range(NEED))
    out_ref[...] = jnp.zeros_like(out_ref)
    sent[0] = above.T
    sent[1] = far.T
    give_next = remote(sent.at[0], landed.at[0], res_send.at[0], res_recv.at[0], me + 1)
    give_skip = remote(sent.at[1], landed.at[1], res_send.at[1], res_recv.at[1], me + skip)

    @pl.when(has_next)
    def _():
        give_next.start()

    @pl.when(has_skip)
    def _():
        give_skip.start()

    out_ref[:, 2 * tile:3 * tile] = diag

    @pl.when(has_next)
    def _():
        out_ref[:, 3 * tile:4 * tile] = above

    @pl.when(jnp.logical_and(has_skip, col == 0))
    def _():
        out_ref[:, 4 * tile:5 * tile] = far

    @pl.when(jnp.logical_and(has_skip, col == 1))
    def _():
        out_ref[:, 0:tile] = far

    for step in range(steps):
        for way in range(2):
            ring(way, step).wait_send()
            share(way, step, col).wait_send()
    share_own(col).wait_send()

    @pl.when(jnp.logical_and(has_back, jnp.logical_not(is_from)))
    def _():
        back_copy.wait_send()

    @pl.when(is_from)
    def _():
        leave_copy.wait_send()

    @pl.when(is_via)
    def _():
        relay_copy.wait_send()

    @pl.when(col == 1)
    def _():
        next_copy.wait_send()

    @pl.when(jnp.logical_and(col == 0, has_skip))
    def _():
        pass_copy.wait_send()

    @pl.when(has_prev)
    def _():
        give_next.wait_recv()
        out_ref[:, tile:2 * tile] = landed[0]

    @pl.when(has_back)
    def _():
        give_skip.wait_recv()

    @pl.when(jnp.logical_and(has_back, col == 0))
    def _():
        out_ref[:, 0:tile] = landed[1]

    @pl.when(jnp.logical_and(has_back, col == 1))
    def _():
        out_ref[:, 4 * tile:5 * tile] = landed[1]

    @pl.when(has_next)
    def _():
        give_next.wait_send()

    @pl.when(has_skip)
    def _():
        give_skip.wait_send()


def ring_body(rows, coefficients, integrals, send_blocks, send_count):
    tile, aux, columns = integrals.shape
    occ = coefficients.shape[1]
    tiles = 2 * rows
    padded = -(-(occ + 8) // LANES) * LANES
    steps = rows - 1
    bf16, f32 = jnp.bfloat16, jnp.float32
    return pl.pallas_call(
        functools.partial(kernel, rows, aux, 1.0 / math.sqrt(aux * occ)),
        out_shape=jax.ShapeDtypeStruct((tile, (2 * BAND + 1) * tile), f32),
        in_specs=[pl.BlockSpec(memory_space=pltpu.HBM)] * 4,
        out_specs=pl.BlockSpec(memory_space=pltpu.VMEM),
        scratch_shapes=[
            pltpu.VMEM((occ, tile), bf16),
            pltpu.VMEM((tile * aux, columns), bf16),
            pltpu.VMEM((send_blocks.shape[2], tiles), jnp.int32),
            pltpu.VMEM((1, tiles), jnp.int32),
            pltpu.VMEM((tiles, padded, tile), bf16),
            pltpu.VMEM((8, tile), f32),
            pltpu.VMEM((NEED, aux * tile, columns), bf16),
            pltpu.VMEM((aux * tile, columns), bf16),
            pltpu.VMEM((columns // LANES, tile * aux, LANES), f32),
            pltpu.VMEM((NEED, columns, padded), bf16),
            pltpu.VMEM((2, tile, tile), f32),
            pltpu.VMEM((2, tile, tile), f32),
            pltpu.SemaphoreType.DMA((4,)),
            pltpu.SemaphoreType.DMA((2, steps)),
            pltpu.SemaphoreType.DMA((2, steps)),
            pltpu.SemaphoreType.DMA((2, steps + 1)),
            pltpu.SemaphoreType.DMA((2, steps + 1)),
            pltpu.SemaphoreType.DMA((3,)),
            pltpu.SemaphoreType.DMA((3,)),
            pltpu.SemaphoreType.DMA((2,)),
            pltpu.SemaphoreType.DMA((2,)),
        ],
        compiler_params=pltpu.CompilerParams(
            collective_id=0, has_side_effects=True, vmem_limit_bytes=60 * 1024 * 1024
        ),
    )(coefficients.T, integrals.reshape(tile * aux, columns), send_blocks[0].T, send_count)


def solution(mesh):
    rows, cols = mesh.shape["row"], mesh.shape["col"]
    if cols == 2 and rows % 2 == 0 and 6 <= rows <= 8:
        body = functools.partial(ring_body, rows)
    else:
        body = general_body
    return jax.shard_map(
        body,
        mesh=mesh,
        in_specs=(
            P(("groups", "row", "col"), None),
            P(("groups", "row", "col"), None, None),
            P(("groups", "row", "col"), None, None),
            P(("groups", "row", "col"), None),
        ),
        out_specs=P(("groups", "row", "col"), None),
        check_vma=False,
    )
```

```python
import functools
import math

import jax
import jax.numpy as jnp
from jax import lax
from jax.experimental import pallas as pl
from jax.experimental.pallas import tpu as pltpu
from jax.sharding import PartitionSpec as P

KB = 8
BAND = 2
LANES = 128
PARTS = 2
NEED = 3


def from_behind(array, axis, by):
    devices = lax.axis_size(axis)
    pairs = [(i, i + by) for i in range(devices) if 0 <= i + by < devices]
    return lax.ppermute(array, axis, pairs)


def pair_block(left_rows, right_rows, norm_scale):
    product = lax.dot_general(
        left_rows, right_rows, (((1,), (1,)), ((), ())), preferred_element_type=jnp.float32
    )
    return product * norm_scale


def general_body(coefficients, integrals, send_blocks, send_count):
    tile_rows = integrals.shape[0]
    aux_count = integrals.shape[1]
    column_total = integrals.shape[2]
    occ_count = coefficients.shape[1]
    slot_count = send_blocks.shape[2]
    owned_blocks = coefficients.reshape(tile_rows // KB, KB, occ_count)
    picked = jnp.take(owned_blocks, send_blocks[0], axis=0)
    live_mask = jnp.arange(slot_count, dtype=jnp.int32)[None, :] < send_count[0][:, None]
    outgoing = jnp.where(live_mask[:, :, None, None], picked, jnp.zeros((), picked.dtype))
    incoming = lax.all_to_all(outgoing, ("row", "col"), split_axis=0, concat_axis=0, tiled=True)
    received = incoming.reshape(column_total, occ_count)
    product = jnp.dot(
        integrals.reshape(tile_rows * aux_count, column_total),
        received,
        preferred_element_type=jnp.float32,
    )
    half_tiles = product.astype(jnp.bfloat16).reshape(tile_rows, aux_count * occ_count)
    norm_scale = 1.0 / math.sqrt(aux_count * occ_count)
    upper_blocks = []
    lower_blocks = []
    for offset in range(1, BAND + 1):
        above_tiles = from_behind(half_tiles, ("row", "col"), -offset)
        upper_blocks.append(pair_block(half_tiles, above_tiles, norm_scale))
        below_tiles = from_behind(half_tiles, ("row", "col"), offset)
        lower_blocks.append(pair_block(half_tiles, below_tiles, norm_scale))
    diagonal = pair_block(half_tiles, half_tiles, norm_scale)
    banded = jnp.concatenate(lower_blocks[::-1] + [diagonal] + upper_blocks, axis=1)
    return banded


def kernel(
    rows, aux, scale,
    coef_hbm, ints_hbm, blocks_hbm, count_hbm, out_ref,
    coef_ref, ints_ref, blocks_ref, count_ref, coefs, notes, held, relay, stage, picked, sent, landed,
    in_sem, ring_send, ring_recv, pair_send, pair_recv, int_send, int_recv, res_send, res_recv,
):
    fetches = [
        pltpu.make_async_copy(src, dst, in_sem.at[k])
        for k, (src, dst) in enumerate((
            (coef_hbm, coef_ref), (blocks_hbm, blocks_ref), (count_hbm, count_ref), (ints_hbm, ints_ref)
        ))
    ]
    for fetch in fetches:
        fetch.start()
    occ = coef_hbm.shape[0]
    tiles = 2 * rows
    depth = rows // 2
    steps = rows - 1
    row, col = lax.axis_index("row"), lax.axis_index("col")
    me = 2 * row + col
    spot = jnp.where(row % 2 == 0, row // 2, rows - 1 - row // 2)
    padded = coefs.shape[1]
    part_rows = padded // PARTS
    tile = coef_ref.shape[1]
    own_rows = tile // KB

    def row_at(where):
        where = lax.rem(where + 2 * rows, rows)
        return jnp.where(where < depth, 2 * where, 2 * (rows - 1 - where) + 1)

    def device(which):
        return {"row": which // 2, "col": which % 2}

    partner = 2 * row + 1 - col
    right = 2 * row_at(spot + 1) + col
    left = 2 * row_at(spot - 1) + col
    skip = jnp.where(col == 0, 2, -2)
    others = (me, me + 1, me + skip)
    has_next = me + 1 < tiles
    has_prev = me >= 1
    has_skip = jnp.logical_and(me + skip >= 0, me + skip < tiles)
    has_back = jnp.logical_and(me - skip >= 0, me - skip < tiles)

    barrier = pltpu.get_barrier_semaphore()

    def greet(which):
        pl.semaphore_signal(
            barrier, inc=1, device_id=device(which), device_id_type=pl.DeviceIdType.MESH
        )

    cross = me - 1 + 2 * col
    has_cross = jnp.logical_and(cross >= 0, cross < tiles)
    for which in (left, right, partner):
        greet(which)
    for there, which in ((has_skip, me + skip), (has_back, me - skip), (has_cross, cross)):
        pl.when(there)(functools.partial(greet, which))

    for fetch in fetches[:3]:
        fetch.wait()
    slots, dests = blocks_ref.shape
    whole = occ // 16 * 16
    live = lax.broadcasted_iota(jnp.int32, (slots, dests), 0) < count_ref[...]
    notes[...] = jnp.zeros_like(notes)
    notes[0:slots, 0:dests] = jnp.where(live, blocks_ref[...], -1).astype(jnp.float32)
    coefs[me, 0:whole] = coef_ref[0:whole]
    rest = jnp.concatenate(
        [
            coef_ref[whole:occ].astype(jnp.float32),
            jnp.zeros((padded - 8 - occ, tile), jnp.float32),
            notes[...],
        ],
        axis=0,
    )
    coefs[me, whole:padded] = rest.astype(coefs.dtype)
    greeted = 3 + has_skip.astype(jnp.int32) + has_back.astype(jnp.int32) + has_cross.astype(jnp.int32)
    pl.semaphore_wait(barrier, greeted)

    def remote(src, dst, send_sem, recv_sem, which):
        return pltpu.make_async_remote_copy(
            src_ref=src, dst_ref=dst, send_sem=send_sem, recv_sem=recv_sem,
            device_id=device(which), device_id_type=pl.DeviceIdType.MESH,
        )

    def piece(owner, part):
        return coefs.at[owner, pl.ds(part * part_rows, part_rows)]

    def ring(way, step):
        back = -(step // 2) if way == 0 else step // 2
        part = step % 2 if way == 0 else 1 - step % 2
        ref = piece(2 * row_at(spot + back) + col, part)
        return remote(ref, ref, ring_send.at[way, step], ring_recv.at[way, step], right if way == 0 else left)

    def arrival(way, step):
        back = -(step // 2) - 1 if way == 0 else step // 2 + 1
        part = step % 2 if way == 0 else 1 - step % 2
        ref = piece(2 * row_at(spot + back) + col, part)
        return remote(ref, ref, ring_send.at[way, step], ring_recv.at[way, step], right if way == 0 else left)

    def share(way, step, core):
        back = -(step // 2) - 1 if way == 0 else step // 2 + 1
        part = step % 2 if way == 0 else 1 - step % 2
        ref = piece(2 * row_at(spot + back) + core, part)
        return remote(ref, ref, pair_send.at[way, step], pair_recv.at[way, step], partner)

    def share_own(core):
        ref = coefs.at[2 * row + core]
        return remote(ref, ref, pair_send.at[0, steps], pair_recv.at[0, steps], partner)

    for step in range(2):
        for way in range(2):
            ring(way, step).start()
    share_own(col).start()

    fetches[3].wait()
    for q in range(ints_ref.shape[1] // LANES):
        stage[q] = ints_ref[:, q * LANES:(q + 1) * LANES].astype(jnp.float32)
        for p in range(aux):
            lines = stage[q, pl.ds(p, tile, stride=aux), :]
            held[0, p * tile:(p + 1) * tile, q * LANES:(q + 1) * LANES] = lines.astype(held.dtype)

    back_copy = remote(held.at[0], held.at[2], int_send.at[0], int_recv.at[1], me - skip)
    next_copy = remote(held.at[0], held.at[1], int_send.at[1], int_recv.at[0], partner)
    pass_copy = remote(held.at[2], held.at[1], int_send.at[1], int_recv.at[0], partner)

    detours = ((4, 6, 2), (tiles - 5, tiles - 7, tiles - 3))
    is_from = functools.reduce(jnp.logical_or, [me == way[0] for way in detours])
    is_via = functools.reduce(jnp.logical_or, [me == way[1] for way in detours])
    via = jnp.where(col == 0, detours[0][1], detours[1][1])
    end = jnp.where(col == 0, detours[0][2], detours[1][2])
    leave_copy = remote(held.at[0], relay, int_send.at[0], int_recv.at[2], via)
    relay_copy = remote(relay, held.at[2], int_send.at[2], int_recv.at[1], end)

    @pl.when(jnp.logical_and(has_back, jnp.logical_not(is_from)))
    def _():
        back_copy.start()

    @pl.when(is_from)
    def _():
        leave_copy.start()

    @pl.when(col == 1)
    def _():
        next_copy.start()

    height = 2 * KB
    lane = lax.broadcasted_iota(jnp.int32, (height, LANES), 1)
    line = lax.broadcasted_iota(jnp.int32, (height, LANES), 0)
    number = lax.broadcasted_iota(jnp.int32, (NEED * height, LANES), 1).astype(jnp.float32)
    inner = (lax.broadcasted_iota(jnp.int32, (NEED * height, LANES), 0) % KB).astype(jnp.float32)
    occ_lane = lax.broadcasted_iota(jnp.int32, (NEED * height, LANES), 1)
    last = padded - LANES

    def pick(owner):
        meta = coefs[owner, pl.ds(padded - 16, 16), :].astype(jnp.float32)
        first = jnp.broadcast_to(meta[8:9], (height, LANES))
        second = jnp.broadcast_to(meta[9:10], (height, LANES))
        both = jnp.where(line < KB, first, second)
        chosen = jnp.concatenate(
            [
                jnp.sum(jnp.where(lane == other, both, 0.0), axis=1, keepdims=True)
                for other in others
            ],
            axis=0,
        )
        hot = (number == chosen * KB + inner).astype(jnp.float32).astype(coefs.dtype)
        got = lax.dot_general(
            hot, coefs[owner], (((1,), (1,)), ((), ())), preferred_element_type=jnp.float32
        )
        tail = jnp.where(occ_lane + last < occ, got[:, last:], 0.0)
        got = got.astype(picked.dtype)
        tail = tail.astype(picked.dtype)
        for k in range(NEED):
            rows_of = pl.ds(pl.multiple_of(owner * height, height), height)
            picked[k, rows_of, 0:last] = got[k * height:(k + 1) * height, 0:last]
            picked[k, rows_of, last:padded] = tail[k * height:(k + 1) * height]

    pick(me)
    for step in range(steps):
        for way in range(2):
            arrival(way, step).wait_recv()
            if step + 2 < steps:
                ring(way, step + 2).start()
            share(way, step, col).start()
        if step == 3:
            @pl.when(is_via)
            def _():
                leave_copy.wait_recv()
                relay_copy.start()
        if step == 0:
            share_own(1 - col).wait_recv()
            pick(partner)
        if step % 2 == 1:
            for way in range(2):
                back = -(step // 2) - 1 if way == 0 else step // 2 + 1
                pick(2 * row_at(spot + back) + col)
            for way in range(2):
                for earlier in (step - 1, step):
                    share(way, earlier, 1 - col).wait_recv()
                back = -(step // 2) - 1 if way == 0 else step // 2 + 1
                pick(2 * row_at(spot + back) + 1 - col)
    opposite = row_at(spot + depth)
    pick(2 * opposite + col)

    @pl.when(has_skip)
    def _():
        remote(held.at[0], held.at[2], int_send.at[0], int_recv.at[1], me - skip).wait_recv()

    @pl.when(jnp.logical_and(col == 0, has_skip))
    def _():
        pass_copy.start()

    for way in range(2):
        share(way, steps - 1, 1 - col).wait_recv()
    pick(2 * opposite + 1 - col)

    @pl.when(has_next)
    def _():
        next_copy.wait_recv()

    group = 2

    def add_up(step, total):
        rows_of = pl.ds(pl.multiple_of(step * group * tile, group * tile), group * tile)
        halves = [
            jnp.dot(
                held[k, rows_of], picked[k], preferred_element_type=jnp.float32
            ).astype(jnp.bfloat16)
            for k in range(NEED)
        ]
        for p in range(group):
            slices = [half[p * tile:(p + 1) * tile] for half in halves]
            total = total + lax.dot_general(
                slices[0], jnp.concatenate(slices, axis=0),
                (((1,), (1,)), ((), ())), preferred_element_type=jnp.float32,
            )
        return total

    zero = jnp.zeros((tile, NEED * tile), jnp.float32)
    total = lax.fori_loop(0, aux // group, add_up, zero) * scale
    diag, above, far = (total[:, k * tile:(k + 1) * tile] for k in range(NEED))
    out_ref[...] = jnp.zeros_like(out_ref)
    sent[0] = above.T
    sent[1] = far.T
    give_next = remote(sent.at[0], landed.at[0], res_send.at[0], res_recv.at[0], me + 1)
    give_skip = remote(sent.at[1], landed.at[1], res_send.at[1], res_recv.at[1], me + skip)

    @pl.when(has_next)
    def _():
        give_next.start()

    @pl.when(has_skip)
    def _():
        give_skip.start()

    out_ref[:, 2 * tile:3 * tile] = diag

    @pl.when(has_next)
    def _():
        out_ref[:, 3 * tile:4 * tile] = above

    @pl.when(jnp.logical_and(has_skip, col == 0))
    def _():
        out_ref[:, 4 * tile:5 * tile] = far

    @pl.when(jnp.logical_and(has_skip, col == 1))
    def _():
        out_ref[:, 0:tile] = far

    for step in range(steps):
        for way in range(2):
            ring(way, step).wait_send()
            share(way, step, col).wait_send()
    share_own(col).wait_send()

    @pl.when(jnp.logical_and(has_back, jnp.logical_not(is_from)))
    def _():
        back_copy.wait_send()

    @pl.when(is_from)
    def _():
        leave_copy.wait_send()

    @pl.when(is_via)
    def _():
        relay_copy.wait_send()

    @pl.when(col == 1)
    def _():
        next_copy.wait_send()

    @pl.when(jnp.logical_and(col == 0, has_skip))
    def _():
        pass_copy.wait_send()

    @pl.when(has_prev)
    def _():
        give_next.wait_recv()
        out_ref[:, tile:2 * tile] = landed[0]

    @pl.when(has_back)
    def _():
        give_skip.wait_recv()

    @pl.when(jnp.logical_and(has_back, col == 0))
    def _():
        out_ref[:, 0:tile] = landed[1]

    @pl.when(jnp.logical_and(has_back, col == 1))
    def _():
        out_ref[:, 4 * tile:5 * tile] = landed[1]

    @pl.when(has_next)
    def _():
        give_next.wait_send()

    @pl.when(has_skip)
    def _():
        give_skip.wait_send()


def ring_body(rows, coefficients, integrals, send_blocks, send_count):
    tile, aux, columns = integrals.shape
    occ = coefficients.shape[1]
    tiles = 2 * rows
    padded = -(-(occ + 8) // LANES) * LANES
    steps = rows - 1
    bf16, f32 = jnp.bfloat16, jnp.float32
    return pl.pallas_call(
        functools.partial(kernel, rows, aux, 1.0 / math.sqrt(aux * occ)),
        out_shape=jax.ShapeDtypeStruct((tile, (2 * BAND + 1) * tile), f32),
        in_specs=[pl.BlockSpec(memory_space=pltpu.HBM)] * 4,
        out_specs=pl.BlockSpec(memory_space=pltpu.VMEM),
        scratch_shapes=[
            pltpu.VMEM((occ, tile), bf16),
            pltpu.VMEM((tile * aux, columns), bf16),
            pltpu.VMEM((send_blocks.shape[2], tiles), jnp.int32),
            pltpu.VMEM((1, tiles), jnp.int32),
            pltpu.VMEM((tiles, padded, tile), bf16),
            pltpu.VMEM((8, tile), f32),
            pltpu.VMEM((NEED, aux * tile, columns), bf16),
            pltpu.VMEM((aux * tile, columns), bf16),
            pltpu.VMEM((columns // LANES, tile * aux, LANES), f32),
            pltpu.VMEM((NEED, columns, padded), bf16),
            pltpu.VMEM((2, tile, tile), f32),
            pltpu.VMEM((2, tile, tile), f32),
            pltpu.SemaphoreType.DMA((4,)),
            pltpu.SemaphoreType.DMA((2, steps)),
            pltpu.SemaphoreType.DMA((2, steps)),
            pltpu.SemaphoreType.DMA((2, steps + 1)),
            pltpu.SemaphoreType.DMA((2, steps + 1)),
            pltpu.SemaphoreType.DMA((3,)),
            pltpu.SemaphoreType.DMA((3,)),
            pltpu.SemaphoreType.DMA((2,)),
            pltpu.SemaphoreType.DMA((2,)),
        ],
        compiler_params=pltpu.CompilerParams(
            collective_id=0, has_side_effects=True, vmem_limit_bytes=60 * 1024 * 1024
        ),
    )(coefficients.T, integrals.reshape(tile * aux, columns), send_blocks[0].T, send_count)


def solution(mesh):
    rows, cols = mesh.shape["row"], mesh.shape["col"]
    if cols == 2 and rows % 2 == 0 and 6 <= rows <= 8:
        body = functools.partial(ring_body, rows)
    else:
        body = general_body
    return jax.shard_map(
        body,
        mesh=mesh,
        in_specs=(
            P(("groups", "row", "col"), None),
            P(("groups", "row", "col"), None, None),
            P(("groups", "row", "col"), None, None),
            P(("groups", "row", "col"), None),
        ),
        out_specs=P(("groups", "row", "col"), None),
        check_vma=False,
    )
```

```python
import functools
import math

import jax
import jax.numpy as jnp
from jax import lax
from jax.experimental import pallas as pl
from jax.experimental.pallas import tpu as pltpu
from jax.sharding import PartitionSpec as P

KB = 8
BAND = 2
LANES = 128
PARTS = 2
NEED = 3


def from_behind(array, axis, by):
    devices = lax.axis_size(axis)
    pairs = [(i, i + by) for i in range(devices) if 0 <= i + by < devices]
    return lax.ppermute(array, axis, pairs)


def pair_block(left_rows, right_rows, norm_scale):
    product = lax.dot_general(
        left_rows, right_rows, (((1,), (1,)), ((), ())), preferred_element_type=jnp.float32
    )
    return product * norm_scale


def general_body(coefficients, integrals, send_blocks, send_count):
    tile_rows = integrals.shape[0]
    aux_count = integrals.shape[1]
    column_total = integrals.shape[2]
    occ_count = coefficients.shape[1]
    slot_count = send_blocks.shape[2]
    owned_blocks = coefficients.reshape(tile_rows // KB, KB, occ_count)
    picked = jnp.take(owned_blocks, send_blocks[0], axis=0)
    live_mask = jnp.arange(slot_count, dtype=jnp.int32)[None, :] < send_count[0][:, None]
    outgoing = jnp.where(live_mask[:, :, None, None], picked, jnp.zeros((), picked.dtype))
    incoming = lax.all_to_all(outgoing, ("row", "col"), split_axis=0, concat_axis=0, tiled=True)
    received = incoming.reshape(column_total, occ_count)
    product = jnp.dot(
        integrals.reshape(tile_rows * aux_count, column_total),
        received,
        preferred_element_type=jnp.float32,
    )
    half_tiles = product.astype(jnp.bfloat16).reshape(tile_rows, aux_count * occ_count)
    norm_scale = 1.0 / math.sqrt(aux_count * occ_count)
    upper_blocks = []
    lower_blocks = []
    for offset in range(1, BAND + 1):
        above_tiles = from_behind(half_tiles, ("row", "col"), -offset)
        upper_blocks.append(pair_block(half_tiles, above_tiles, norm_scale))
        below_tiles = from_behind(half_tiles, ("row", "col"), offset)
        lower_blocks.append(pair_block(half_tiles, below_tiles, norm_scale))
    diagonal = pair_block(half_tiles, half_tiles, norm_scale)
    banded = jnp.concatenate(lower_blocks[::-1] + [diagonal] + upper_blocks, axis=1)
    return banded


def kernel(
    rows, aux, scale,
    coef_hbm, ints_hbm, blocks_hbm, count_hbm, out_ref,
    coef_ref, ints_ref, blocks_ref, count_ref, coefs, notes, held, relay, stage, picked, sent, landed,
    in_sem, ring_send, ring_recv, pair_send, pair_recv, int_send, int_recv, res_send, res_recv,
):
    fetches = [
        pltpu.make_async_copy(src, dst, in_sem.at[k])
        for k, (src, dst) in enumerate((
            (coef_hbm, coef_ref), (blocks_hbm, blocks_ref), (count_hbm, count_ref), (ints_hbm, ints_ref)
        ))
    ]
    for fetch in fetches:
        fetch.start()
    occ = coef_hbm.shape[0]
    tiles = 2 * rows
    depth = rows // 2
    steps = rows - 1
    row, col = lax.axis_index("row"), lax.axis_index("col")
    me = 2 * row + col
    spot = jnp.where(row % 2 == 0, row // 2, rows - 1 - row // 2)
    padded = coefs.shape[1]
    part_rows = padded // PARTS
    tile = coef_ref.shape[1]
    own_rows = tile // KB

    def row_at(where):
        where = lax.rem(where + 2 * rows, rows)
        return jnp.where(where < depth, 2 * where, 2 * (rows - 1 - where) + 1)

    def device(which):
        return {"row": which // 2, "col": which % 2}

    partner = 2 * row + 1 - col
    right = 2 * row_at(spot + 1) + col
    left = 2 * row_at(spot - 1) + col
    skip = jnp.where(col == 0, 2, -2)
    others = (me, me + 1, me + skip)
    has_next = me + 1 < tiles
    has_prev = me >= 1
    has_skip = jnp.logical_and(me + skip >= 0, me + skip < tiles)
    has_back = jnp.logical_and(me - skip >= 0, me - skip < tiles)

    barrier = pltpu.get_barrier_semaphore()

    def greet(which):
        pl.semaphore_signal(
            barrier, inc=1, device_id=device(which), device_id_type=pl.DeviceIdType.MESH
        )

    cross = me - 1 + 2 * col
    has_cross = jnp.logical_and(cross >= 0, cross < tiles)
    for which in (left, right, partner):
        greet(which)
    for there, which in ((has_skip, me + skip), (has_back, me - skip), (has_cross, cross)):
        pl.when(there)(functools.partial(greet, which))

    for fetch in fetches[:3]:
        fetch.wait()
    slots, dests = blocks_ref.shape
    whole = occ // 16 * 16
    live = lax.broadcasted_iota(jnp.int32, (slots, dests), 0) < count_ref[...]
    notes[...] = jnp.zeros_like(notes)
    notes[0:slots, 0:dests] = jnp.where(live, blocks_ref[...], -1).astype(jnp.float32)
    coefs[me, 0:whole] = coef_ref[0:whole]
    rest = jnp.concatenate(
        [
            coef_ref[whole:occ].astype(jnp.float32),
            jnp.zeros((padded - 8 - occ, tile), jnp.float32),
            notes[...],
        ],
        axis=0,
    )
    coefs[me, whole:padded] = rest.astype(coefs.dtype)
    greeted = 3 + has_skip.astype(jnp.int32) + has_back.astype(jnp.int32) + has_cross.astype(jnp.int32)
    fetches[3].wait()
    for q in range(ints_ref.shape[1] // LANES):
        stage[q] = ints_ref[:, q * LANES:(q + 1) * LANES].astype(jnp.float32)
        for p in range(aux):
            lines = stage[q, pl.ds(p, tile, stride=aux), :]
            held[0, p * tile:(p + 1) * tile, q * LANES:(q + 1) * LANES] = lines.astype(held.dtype)

    pl.semaphore_wait(barrier, greeted)

    def remote(src, dst, send_sem, recv_sem, which):
        return pltpu.make_async_remote_copy(
            src_ref=src, dst_ref=dst, send_sem=send_sem, recv_sem=recv_sem,
            device_id=device(which), device_id_type=pl.DeviceIdType.MESH,
        )

    def piece(owner, part):
        return coefs.at[owner, pl.ds(part * part_rows, part_rows)]

    def ring(way, step):
        back = -(step // 2) if way == 0 else step // 2
        part = step % 2 if way == 0 else 1 - step % 2
        ref = piece(2 * row_at(spot + back) + col, part)
        return remote(ref, ref, ring_send.at[way, step], ring_recv.at[way, step], right if way == 0 else left)

    def arrival(way, step):
        back = -(step // 2) - 1 if way == 0 else step // 2 + 1
        part = step % 2 if way == 0 else 1 - step % 2
        ref = piece(2 * row_at(spot + back) + col, part)
        return remote(ref, ref, ring_send.at[way, step], ring_recv.at[way, step], right if way == 0 else left)

    def share(way, step, core):
        back = -(step // 2) - 1 if way == 0 else step // 2 + 1
        part = step % 2 if way == 0 else 1 - step % 2
        ref = piece(2 * row_at(spot + back) + core, part)
        return remote(ref, ref, pair_send.at[way, step], pair_recv.at[way, step], partner)

    def share_own(core):
        ref = coefs.at[2 * row + core]
        return remote(ref, ref, pair_send.at[0, steps], pair_recv.at[0, steps], partner)

    for step in range(2):
        for way in range(2):
            ring(way, step).start()
    share_own(col).start()

    back_copy = remote(held.at[0], held.at[2], int_send.at[0], int_recv.at[1], me - skip)
    next_copy = remote(held.at[0], held.at[1], int_send.at[1], int_recv.at[0], partner)
    pass_copy = remote(held.at[2], held.at[1], int_send.at[1], int_recv.at[0], partner)

    detours = ((4, 6, 2), (tiles - 5, tiles - 7, tiles - 3))
    is_from = functools.reduce(jnp.logical_or, [me == way[0] for way in detours])
    is_via = functools.reduce(jnp.logical_or, [me == way[1] for way in detours])
    via = jnp.where(col == 0, detours[0][1], detours[1][1])
    end = jnp.where(col == 0, detours[0][2], detours[1][2])
    leave_copy = remote(held.at[0], relay, int_send.at[0], int_recv.at[2], via)
    relay_copy = remote(relay, held.at[2], int_send.at[2], int_recv.at[1], end)

    @pl.when(jnp.logical_and(has_back, jnp.logical_not(is_from)))
    def _():
        back_copy.start()

    @pl.when(is_from)
    def _():
        leave_copy.start()

    @pl.when(col == 1)
    def _():
        next_copy.start()

    height = 2 * KB
    lane = lax.broadcasted_iota(jnp.int32, (height, LANES), 1)
    line = lax.broadcasted_iota(jnp.int32, (height, LANES), 0)
    number = lax.broadcasted_iota(jnp.int32, (NEED * height, LANES), 1).astype(jnp.float32)
    inner = (lax.broadcasted_iota(jnp.int32, (NEED * height, LANES), 0) % KB).astype(jnp.float32)
    occ_lane = lax.broadcasted_iota(jnp.int32, (NEED * height, LANES), 1)
    last = padded - LANES

    def pick(owner):
        meta = coefs[owner, pl.ds(padded - 16, 16), :].astype(jnp.float32)
        first = jnp.broadcast_to(meta[8:9], (height, LANES))
        second = jnp.broadcast_to(meta[9:10], (height, LANES))
        both = jnp.where(line < KB, first, second)
        chosen = jnp.concatenate(
            [
                jnp.sum(jnp.where(lane == other, both, 0.0), axis=1, keepdims=True)
                for other in others
            ],
            axis=0,
        )
        hot = (number == chosen * KB + inner).astype(jnp.float32).astype(coefs.dtype)
        got = lax.dot_general(
            hot, coefs[owner], (((1,), (1,)), ((), ())), preferred_element_type=jnp.float32
        )
        tail = jnp.where(occ_lane + last < occ, got[:, last:], 0.0)
        got = got.astype(picked.dtype)
        tail = tail.astype(picked.dtype)
        for k in range(NEED):
            rows_of = pl.ds(pl.multiple_of(owner * height, height), height)
            picked[k, rows_of, 0:last] = got[k * height:(k + 1) * height, 0:last]
            picked[k, rows_of, last:padded] = tail[k * height:(k + 1) * height]

    pick(me)
    for step in range(steps):
        for way in range(2):
            arrival(way, step).wait_recv()
            if step + 2 < steps:
                ring(way, step + 2).start()
            share(way, step, col).start()
        if step == 3:
            @pl.when(is_via)
            def _():
                leave_copy.wait_recv()
                relay_copy.start()
        if step == 0:
            share_own(1 - col).wait_recv()
            pick(partner)
        if step % 2 == 1:
            for way in range(2):
                back = -(step // 2) - 1 if way == 0 else step // 2 + 1
                pick(2 * row_at(spot + back) + col)
            for way in range(2):
                for earlier in (step - 1, step):
                    share(way, earlier, 1 - col).wait_recv()
                back = -(step // 2) - 1 if way == 0 else step // 2 + 1
                pick(2 * row_at(spot + back) + 1 - col)
    opposite = row_at(spot + depth)
    pick(2 * opposite + col)

    @pl.when(has_skip)
    def _():
        remote(held.at[0], held.at[2], int_send.at[0], int_recv.at[1], me - skip).wait_recv()

    @pl.when(jnp.logical_and(col == 0, has_skip))
    def _():
        pass_copy.start()

    for way in range(2):
        share(way, steps - 1, 1 - col).wait_recv()
    pick(2 * opposite + 1 - col)

    @pl.when(has_next)
    def _():
        next_copy.wait_recv()

    group = 4

    def add_up(step, total):
        rows_of = pl.ds(pl.multiple_of(step * group * tile, group * tile), group * tile)
        halves = [
            jnp.dot(
                held[k, rows_of], picked[k], preferred_element_type=jnp.float32
            ).astype(jnp.bfloat16)
            for k in range(NEED)
        ]
        for p in range(group):
            slices = [half[p * tile:(p + 1) * tile] for half in halves]
            total = total + lax.dot_general(
                slices[0], jnp.concatenate(slices, axis=0),
                (((1,), (1,)), ((), ())), preferred_element_type=jnp.float32,
            )
        return total

    zero = jnp.zeros((tile, NEED * tile), jnp.float32)
    total = lax.fori_loop(0, aux // group, add_up, zero) * scale
    diag, above, far = (total[:, k * tile:(k + 1) * tile] for k in range(NEED))
    out_ref[...] = jnp.zeros_like(out_ref)
    sent[0] = above.T
    sent[1] = far.T
    give_next = remote(sent.at[0], landed.at[0], res_send.at[0], res_recv.at[0], me + 1)
    give_skip = remote(sent.at[1], landed.at[1], res_send.at[1], res_recv.at[1], me + skip)

    @pl.when(has_next)
    def _():
        give_next.start()

    @pl.when(has_skip)
    def _():
        give_skip.start()

    out_ref[:, 2 * tile:3 * tile] = diag

    @pl.when(has_next)
    def _():
        out_ref[:, 3 * tile:4 * tile] = above

    @pl.when(jnp.logical_and(has_skip, col == 0))
    def _():
        out_ref[:, 4 * tile:5 * tile] = far

    @pl.when(jnp.logical_and(has_skip, col == 1))
    def _():
        out_ref[:, 0:tile] = far

    for step in range(steps):
        for way in range(2):
            ring(way, step).wait_send()
            share(way, step, col).wait_send()
    share_own(col).wait_send()

    @pl.when(jnp.logical_and(has_back, jnp.logical_not(is_from)))
    def _():
        back_copy.wait_send()

    @pl.when(is_from)
    def _():
        leave_copy.wait_send()

    @pl.when(is_via)
    def _():
        relay_copy.wait_send()

    @pl.when(col == 1)
    def _():
        next_copy.wait_send()

    @pl.when(jnp.logical_and(col == 0, has_skip))
    def _():
        pass_copy.wait_send()

    @pl.when(has_prev)
    def _():
        give_next.wait_recv()
        out_ref[:, tile:2 * tile] = landed[0]

    @pl.when(has_back)
    def _():
        give_skip.wait_recv()

    @pl.when(jnp.logical_and(has_back, col == 0))
    def _():
        out_ref[:, 0:tile] = landed[1]

    @pl.when(jnp.logical_and(has_back, col == 1))
    def _():
        out_ref[:, 4 * tile:5 * tile] = landed[1]

    @pl.when(has_next)
    def _():
        give_next.wait_send()

    @pl.when(has_skip)
    def _():
        give_skip.wait_send()


def ring_body(rows, coefficients, integrals, send_blocks, send_count):
    tile, aux, columns = integrals.shape
    occ = coefficients.shape[1]
    tiles = 2 * rows
    padded = -(-(occ + 8) // LANES) * LANES
    steps = rows - 1
    bf16, f32 = jnp.bfloat16, jnp.float32
    return pl.pallas_call(
        functools.partial(kernel, rows, aux, 1.0 / math.sqrt(aux * occ)),
        out_shape=jax.ShapeDtypeStruct((tile, (2 * BAND + 1) * tile), f32),
        in_specs=[pl.BlockSpec(memory_space=pltpu.HBM)] * 4,
        out_specs=pl.BlockSpec(memory_space=pltpu.VMEM),
        scratch_shapes=[
            pltpu.VMEM((occ, tile), bf16),
            pltpu.VMEM((tile * aux, columns), bf16),
            pltpu.VMEM((send_blocks.shape[2], tiles), jnp.int32),
            pltpu.VMEM((1, tiles), jnp.int32),
            pltpu.VMEM((tiles, padded, tile), bf16),
            pltpu.VMEM((8, tile), f32),
            pltpu.VMEM((NEED, aux * tile, columns), bf16),
            pltpu.VMEM((aux * tile, columns), bf16),
            pltpu.VMEM((columns // LANES, tile * aux, LANES), f32),
            pltpu.VMEM((NEED, columns, padded), bf16),
            pltpu.VMEM((2, tile, tile), f32),
            pltpu.VMEM((2, tile, tile), f32),
            pltpu.SemaphoreType.DMA((4,)),
            pltpu.SemaphoreType.DMA((2, steps)),
            pltpu.SemaphoreType.DMA((2, steps)),
            pltpu.SemaphoreType.DMA((2, steps + 1)),
            pltpu.SemaphoreType.DMA((2, steps + 1)),
            pltpu.SemaphoreType.DMA((3,)),
            pltpu.SemaphoreType.DMA((3,)),
            pltpu.SemaphoreType.DMA((2,)),
            pltpu.SemaphoreType.DMA((2,)),
        ],
        compiler_params=pltpu.CompilerParams(
            collective_id=0, has_side_effects=True, vmem_limit_bytes=60 * 1024 * 1024
        ),
    )(coefficients.T, integrals.reshape(tile * aux, columns), send_blocks[0].T, send_count)


def solution(mesh):
    rows, cols = mesh.shape["row"], mesh.shape["col"]
    if cols == 2 and rows % 2 == 0 and 6 <= rows <= 8:
        body = functools.partial(ring_body, rows)
    else:
        body = general_body
    return jax.shard_map(
        body,
        mesh=mesh,
        in_specs=(
            P(("groups", "row", "col"), None),
            P(("groups", "row", "col"), None, None),
            P(("groups", "row", "col"), None, None),
            P(("groups", "row", "col"), None),
        ),
        out_specs=P(("groups", "row", "col"), None),
        check_vma=False,
    )
```

```python
import functools
import math

import jax
import jax.numpy as jnp
from jax import lax
from jax.experimental import pallas as pl
from jax.experimental.pallas import tpu as pltpu
from jax.sharding import PartitionSpec as P

KB = 8
BAND = 2
LANES = 128
PARTS = 2
NEED = 3


def from_behind(array, axis, by):
    devices = lax.axis_size(axis)
    pairs = [(i, i + by) for i in range(devices) if 0 <= i + by < devices]
    return lax.ppermute(array, axis, pairs)


def pair_block(left_rows, right_rows, norm_scale):
    product = lax.dot_general(
        left_rows, right_rows, (((1,), (1,)), ((), ())), preferred_element_type=jnp.float32
    )
    return product * norm_scale


def general_body(coefficients, integrals, send_blocks, send_count):
    tile_rows = integrals.shape[0]
    aux_count = integrals.shape[1]
    column_total = integrals.shape[2]
    occ_count = coefficients.shape[1]
    slot_count = send_blocks.shape[2]
    owned_blocks = coefficients.reshape(tile_rows // KB, KB, occ_count)
    picked = jnp.take(owned_blocks, send_blocks[0], axis=0)
    live_mask = jnp.arange(slot_count, dtype=jnp.int32)[None, :] < send_count[0][:, None]
    outgoing = jnp.where(live_mask[:, :, None, None], picked, jnp.zeros((), picked.dtype))
    incoming = lax.all_to_all(outgoing, ("row", "col"), split_axis=0, concat_axis=0, tiled=True)
    received = incoming.reshape(column_total, occ_count)
    product = jnp.dot(
        integrals.reshape(tile_rows * aux_count, column_total),
        received,
        preferred_element_type=jnp.float32,
    )
    half_tiles = product.astype(jnp.bfloat16).reshape(tile_rows, aux_count * occ_count)
    norm_scale = 1.0 / math.sqrt(aux_count * occ_count)
    upper_blocks = []
    lower_blocks = []
    for offset in range(1, BAND + 1):
        above_tiles = from_behind(half_tiles, ("row", "col"), -offset)
        upper_blocks.append(pair_block(half_tiles, above_tiles, norm_scale))
        below_tiles = from_behind(half_tiles, ("row", "col"), offset)
        lower_blocks.append(pair_block(half_tiles, below_tiles, norm_scale))
    diagonal = pair_block(half_tiles, half_tiles, norm_scale)
    banded = jnp.concatenate(lower_blocks[::-1] + [diagonal] + upper_blocks, axis=1)
    return banded


def kernel(
    rows, aux, scale,
    coef_hbm, ints_hbm, blocks_hbm, count_hbm, out_ref,
    coef_ref, ints_ref, blocks_ref, count_ref, coefs, notes, held, relay, stage, picked, sent, landed,
    in_sem, ring_send, ring_recv, pair_send, pair_recv, int_send, int_recv, res_send, res_recv,
):
    fetches = [
        pltpu.make_async_copy(src, dst, in_sem.at[k])
        for k, (src, dst) in enumerate((
            (coef_hbm, coef_ref), (blocks_hbm, blocks_ref), (count_hbm, count_ref), (ints_hbm, ints_ref)
        ))
    ]
    for fetch in fetches:
        fetch.start()
    occ = coef_hbm.shape[0]
    tiles = 2 * rows
    depth = rows // 2
    steps = rows - 1
    row, col = lax.axis_index("row"), lax.axis_index("col")
    me = 2 * row + col
    spot = jnp.where(row % 2 == 0, row // 2, rows - 1 - row // 2)
    padded = coefs.shape[1]
    part_rows = padded // PARTS
    tile = coef_ref.shape[1]
    own_rows = tile // KB

    def row_at(where):
        where = lax.rem(where + 2 * rows, rows)
        return jnp.where(where < depth, 2 * where, 2 * (rows - 1 - where) + 1)

    def device(which):
        return {"row": which // 2, "col": which % 2}

    partner = 2 * row + 1 - col
    right = 2 * row_at(spot + 1) + col
    left = 2 * row_at(spot - 1) + col
    skip = jnp.where(col == 0, 2, -2)
    others = (me, me + 1, me + skip)
    has_next = me + 1 < tiles
    has_prev = me >= 1
    has_skip = jnp.logical_and(me + skip >= 0, me + skip < tiles)
    has_back = jnp.logical_and(me - skip >= 0, me - skip < tiles)

    barrier = pltpu.get_barrier_semaphore()

    def greet(which):
        pl.semaphore_signal(
            barrier, inc=1, device_id=device(which), device_id_type=pl.DeviceIdType.MESH
        )

    cross = me - 1 + 2 * col
    has_cross = jnp.logical_and(cross >= 0, cross < tiles)
    for which in (left, right, partner):
        greet(which)
    for there, which in ((has_skip, me + skip), (has_back, me - skip), (has_cross, cross)):
        pl.when(there)(functools.partial(greet, which))

    for fetch in fetches[:3]:
        fetch.wait()
    slots, dests = blocks_ref.shape
    whole = occ // 16 * 16
    live = lax.broadcasted_iota(jnp.int32, (slots, dests), 0) < count_ref[...]
    notes[...] = jnp.zeros_like(notes)
    notes[0:slots, 0:dests] = jnp.where(live, blocks_ref[...], -1).astype(jnp.float32)
    coefs[me, 0:whole] = coef_ref[0:whole]
    rest = jnp.concatenate(
        [
            coef_ref[whole:occ].astype(jnp.float32),
            jnp.zeros((padded - 8 - occ, tile), jnp.float32),
            notes[...],
        ],
        axis=0,
    )
    coefs[me, whole:padded] = rest.astype(coefs.dtype)
    greeted = 3 + has_skip.astype(jnp.int32) + has_back.astype(jnp.int32) + has_cross.astype(jnp.int32)
    out_ref[...] = jnp.zeros_like(out_ref)
    fetches[3].wait()
    for q in range(ints_ref.shape[1] // LANES):
        stage[q] = ints_ref[:, q * LANES:(q + 1) * LANES].astype(jnp.float32)
        for p in range(aux):
            lines = stage[q, pl.ds(p, tile, stride=aux), :]
            held[0, p * tile:(p + 1) * tile, q * LANES:(q + 1) * LANES] = lines.astype(held.dtype)

    pl.semaphore_wait(barrier, greeted)

    def remote(src, dst, send_sem, recv_sem, which):
        return pltpu.make_async_remote_copy(
            src_ref=src, dst_ref=dst, send_sem=send_sem, recv_sem=recv_sem,
            device_id=device(which), device_id_type=pl.DeviceIdType.MESH,
        )

    def piece(owner, part):
        return coefs.at[owner, pl.ds(part * part_rows, part_rows)]

    def ring(way, step):
        back = -(step // 2) if way == 0 else step // 2
        part = step % 2 if way == 0 else 1 - step % 2
        ref = piece(2 * row_at(spot + back) + col, part)
        return remote(ref, ref, ring_send.at[way, step], ring_recv.at[way, step], right if way == 0 else left)

    def arrival(way, step):
        back = -(step // 2) - 1 if way == 0 else step // 2 + 1
        part = step % 2 if way == 0 else 1 - step % 2
        ref = piece(2 * row_at(spot + back) + col, part)
        return remote(ref, ref, ring_send.at[way, step], ring_recv.at[way, step], right if way == 0 else left)

    def share(way, step, core):
        back = -(step // 2) - 1 if way == 0 else step // 2 + 1
        part = step % 2 if way == 0 else 1 - step % 2
        ref = piece(2 * row_at(spot + back) + core, part)
        return remote(ref, ref, pair_send.at[way, step], pair_recv.at[way, step], partner)

    def share_own(core):
        ref = coefs.at[2 * row + core]
        return remote(ref, ref, pair_send.at[0, steps], pair_recv.at[0, steps], partner)

    for step in range(2):
        for way in range(2):
            ring(way, step).start()
    share_own(col).start()

    back_copy = remote(held.at[0], held.at[2], int_send.at[0], int_recv.at[1], me - skip)
    next_copy = remote(held.at[0], held.at[1], int_send.at[1], int_recv.at[0], partner)
    pass_copy = remote(held.at[2], held.at[1], int_send.at[1], int_recv.at[0], partner)

    detours = ((4, 6, 2), (tiles - 5, tiles - 7, tiles - 3))
    is_from = functools.reduce(jnp.logical_or, [me == way[0] for way in detours])
    is_via = functools.reduce(jnp.logical_or, [me == way[1] for way in detours])
    via = jnp.where(col == 0, detours[0][1], detours[1][1])
    end = jnp.where(col == 0, detours[0][2], detours[1][2])
    leave_copy = remote(held.at[0], relay, int_send.at[0], int_recv.at[2], via)
    relay_copy = remote(relay, held.at[2], int_send.at[2], int_recv.at[1], end)

    @pl.when(jnp.logical_and(has_back, jnp.logical_not(is_from)))
    def _():
        back_copy.start()

    @pl.when(is_from)
    def _():
        leave_copy.start()

    @pl.when(col == 1)
    def _():
        next_copy.start()

    height = 2 * KB
    lane = lax.broadcasted_iota(jnp.int32, (height, LANES), 1)
    line = lax.broadcasted_iota(jnp.int32, (height, LANES), 0)
    number = lax.broadcasted_iota(jnp.int32, (NEED * height, LANES), 1).astype(jnp.float32)
    inner = (lax.broadcasted_iota(jnp.int32, (NEED * height, LANES), 0) % KB).astype(jnp.float32)
    occ_lane = lax.broadcasted_iota(jnp.int32, (NEED * height, LANES), 1)
    last = padded - LANES

    def pick(owner):
        meta = coefs[owner, pl.ds(padded - 16, 16), :].astype(jnp.float32)
        first = jnp.broadcast_to(meta[8:9], (height, LANES))
        second = jnp.broadcast_to(meta[9:10], (height, LANES))
        both = jnp.where(line < KB, first, second)
        chosen = jnp.concatenate(
            [
                jnp.sum(jnp.where(lane == other, both, 0.0), axis=1, keepdims=True)
                for other in others
            ],
            axis=0,
        )
        hot = (number == chosen * KB + inner).astype(jnp.float32).astype(coefs.dtype)
        got = lax.dot_general(
            hot, coefs[owner], (((1,), (1,)), ((), ())), preferred_element_type=jnp.float32
        )
        tail = jnp.where(occ_lane + last < occ, got[:, last:], 0.0)
        got = got.astype(picked.dtype)
        tail = tail.astype(picked.dtype)
        for k in range(NEED):
            rows_of = pl.ds(pl.multiple_of(owner * height, height), height)
            picked[k, rows_of, 0:last] = got[k * height:(k + 1) * height, 0:last]
            picked[k, rows_of, last:padded] = tail[k * height:(k + 1) * height]

    pick(me)
    for step in range(steps):
        for way in range(2):
            arrival(way, step).wait_recv()
            if step + 2 < steps:
                ring(way, step + 2).start()
            share(way, step, col).start()
        if step == steps - 2:
            @pl.when(has_skip)
            def _():
                remote(held.at[0], held.at[2], int_send.at[0], int_recv.at[1], me - skip).wait_recv()

            @pl.when(jnp.logical_and(col == 0, has_skip))
            def _():
                pass_copy.start()

        if step == 3:
            @pl.when(is_via)
            def _():
                leave_copy.wait_recv()
                relay_copy.start()
        if step == 0:
            share_own(1 - col).wait_recv()
            pick(partner)
        if step % 2 == 1:
            for way in range(2):
                back = -(step // 2) - 1 if way == 0 else step // 2 + 1
                pick(2 * row_at(spot + back) + col)
            for way in range(2):
                for earlier in (step - 1, step):
                    share(way, earlier, 1 - col).wait_recv()
                back = -(step // 2) - 1 if way == 0 else step // 2 + 1
                pick(2 * row_at(spot + back) + 1 - col)
    opposite = row_at(spot + depth)
    pick(2 * opposite + col)

    for way in range(2):
        share(way, steps - 1, 1 - col).wait_recv()
    pick(2 * opposite + 1 - col)

    @pl.when(has_next)
    def _():
        next_copy.wait_recv()

    group = 4

    def add_up(step, total):
        rows_of = pl.ds(pl.multiple_of(step * group * tile, group * tile), group * tile)
        halves = [
            jnp.dot(
                held[k, rows_of], picked[k], preferred_element_type=jnp.float32
            ).astype(jnp.bfloat16)
            for k in range(NEED)
        ]
        for p in range(group):
            slices = [half[p * tile:(p + 1) * tile] for half in halves]
            total = total + lax.dot_general(
                slices[0], jnp.concatenate(slices, axis=0),
                (((1,), (1,)), ((), ())), preferred_element_type=jnp.float32,
            )
        return total

    zero = jnp.zeros((tile, NEED * tile), jnp.float32)
    total = lax.fori_loop(0, aux // group, add_up, zero) * scale
    diag, above, far = (total[:, k * tile:(k + 1) * tile] for k in range(NEED))
    sent[0] = above.T
    sent[1] = far.T
    give_next = remote(sent.at[0], landed.at[0], res_send.at[0], res_recv.at[0], me + 1)
    give_skip = remote(sent.at[1], landed.at[1], res_send.at[1], res_recv.at[1], me + skip)

    @pl.when(has_next)
    def _():
        give_next.start()

    @pl.when(has_skip)
    def _():
        give_skip.start()

    out_ref[:, 2 * tile:3 * tile] = diag

    @pl.when(has_next)
    def _():
        out_ref[:, 3 * tile:4 * tile] = above

    @pl.when(jnp.logical_and(has_skip, col == 0))
    def _():
        out_ref[:, 4 * tile:5 * tile] = far

    @pl.when(jnp.logical_and(has_skip, col == 1))
    def _():
        out_ref[:, 0:tile] = far

    for step in range(steps):
        for way in range(2):
            ring(way, step).wait_send()
            share(way, step, col).wait_send()
    share_own(col).wait_send()

    @pl.when(jnp.logical_and(has_back, jnp.logical_not(is_from)))
    def _():
        back_copy.wait_send()

    @pl.when(is_from)
    def _():
        leave_copy.wait_send()

    @pl.when(is_via)
    def _():
        relay_copy.wait_send()

    @pl.when(col == 1)
    def _():
        next_copy.wait_send()

    @pl.when(jnp.logical_and(col == 0, has_skip))
    def _():
        pass_copy.wait_send()

    @pl.when(has_prev)
    def _():
        give_next.wait_recv()
        out_ref[:, tile:2 * tile] = landed[0]

    @pl.when(has_back)
    def _():
        give_skip.wait_recv()

    @pl.when(jnp.logical_and(has_back, col == 0))
    def _():
        out_ref[:, 0:tile] = landed[1]

    @pl.when(jnp.logical_and(has_back, col == 1))
    def _():
        out_ref[:, 4 * tile:5 * tile] = landed[1]

    @pl.when(has_next)
    def _():
        give_next.wait_send()

    @pl.when(has_skip)
    def _():
        give_skip.wait_send()


def ring_body(rows, coefficients, integrals, send_blocks, send_count):
    tile, aux, columns = integrals.shape
    occ = coefficients.shape[1]
    tiles = 2 * rows
    padded = -(-(occ + 8) // LANES) * LANES
    steps = rows - 1
    bf16, f32 = jnp.bfloat16, jnp.float32
    return pl.pallas_call(
        functools.partial(kernel, rows, aux, 1.0 / math.sqrt(aux * occ)),
        out_shape=jax.ShapeDtypeStruct((tile, (2 * BAND + 1) * tile), f32),
        in_specs=[pl.BlockSpec(memory_space=pltpu.HBM)] * 4,
        out_specs=pl.BlockSpec(memory_space=pltpu.VMEM),
        scratch_shapes=[
            pltpu.VMEM((occ, tile), bf16),
            pltpu.VMEM((tile * aux, columns), bf16),
            pltpu.VMEM((send_blocks.shape[2], tiles), jnp.int32),
            pltpu.VMEM((1, tiles), jnp.int32),
            pltpu.VMEM((tiles, padded, tile), bf16),
            pltpu.VMEM((8, tile), f32),
            pltpu.VMEM((NEED, aux * tile, columns), bf16),
            pltpu.VMEM((aux * tile, columns), bf16),
            pltpu.VMEM((columns // LANES, tile * aux, LANES), f32),
            pltpu.VMEM((NEED, columns, padded), bf16),
            pltpu.VMEM((2, tile, tile), f32),
            pltpu.VMEM((2, tile, tile), f32),
            pltpu.SemaphoreType.DMA((4,)),
            pltpu.SemaphoreType.DMA((2, steps)),
            pltpu.SemaphoreType.DMA((2, steps)),
            pltpu.SemaphoreType.DMA((2, steps + 1)),
            pltpu.SemaphoreType.DMA((2, steps + 1)),
            pltpu.SemaphoreType.DMA((3,)),
            pltpu.SemaphoreType.DMA((3,)),
            pltpu.SemaphoreType.DMA((2,)),
            pltpu.SemaphoreType.DMA((2,)),
        ],
        compiler_params=pltpu.CompilerParams(
            collective_id=0, has_side_effects=True, vmem_limit_bytes=60 * 1024 * 1024
        ),
    )(coefficients.T, integrals.reshape(tile * aux, columns), send_blocks[0].T, send_count)


def solution(mesh):
    rows, cols = mesh.shape["row"], mesh.shape["col"]
    if cols == 2 and rows % 2 == 0 and 6 <= rows <= 8:
        body = functools.partial(ring_body, rows)
    else:
        body = general_body
    return jax.shard_map(
        body,
        mesh=mesh,
        in_specs=(
            P(("groups", "row", "col"), None),
            P(("groups", "row", "col"), None, None),
            P(("groups", "row", "col"), None, None),
            P(("groups", "row", "col"), None),
        ),
        out_specs=P(("groups", "row", "col"), None),
        check_vma=False,
    )
```
